256 devices in a mesh: section: 16 (over z, core), tensor: 8 (over y_hi, x), group: 2 (over y_lo).
Axes of the slice: x: 4, y: 4 (y_hi: 2, y_lo: 2; y = y_hi * 2 + y_lo), z: 8, core: 2. Of those that a mesh axis runs over, the one named last changes fastest.
Arguments:
- layer_deltas: bfloat16 [32, 256, 16384], P('section', 'group', 'tensor'), may hold values from -6 to 6
- tap_layers: int32 [3], replicated, may hold values from 0 to 31, as said below
- norm_gain: float32 [3, 16384], P(None, 'tensor'), may hold values from 0.1 to 1.9
- fc_weight: bfloat16 [3, 16384, 16384], P(None, 'tensor', ('section', 'group')), may hold values from -0.02734375 to 0.02734375
Outputs:
- joined: bfloat16 [256, 16384], P(None, ('section', 'group'))
The draws below stay inside these ranges and needn't reach their ends.
Inputs may be any that keep to these rules, and one draw needn't show every extreme that they name: `tap_layers`: three layers, strictly rising: low in the first third of the 32 layers, mid in the second, high the last layer.
All inputs are finite; a program needn't handle non-finite values.
Results may differ from the reference program's by a relative error of at most 0.005.
Values may be sent and summed in bfloat16 or wider, within the bound.
No kernel may reach another device: no remote copies, remote signals or barrier semaphores. Data moves between devices by JAX's collectives and lax.ppermute only.
A program may use at most 64 MiB of HBM per device.

```python
import jax
import jax.numpy as jnp
from jax import lax

D = 16384
TAPS = 3
LAYERS = 32
TOKENS = 256


def draw_tap_layers(key, part):
    key = jax.random.fold_in(key, 5)
    keys = jax.random.split(key, 2)
    third = LAYERS // 3
    low = jax.random.randint(keys[0], (), 0, third)
    middle = jax.random.randint(keys[1], (), third, 2 * third)
    high = jnp.array(LAYERS - 1, jnp.int32)
    return jnp.stack([low.astype(jnp.int32), middle.astype(jnp.int32), high]).astype(jnp.int32)


def block_scale(stream_key, shape, shards, least, top_value):
    def one(dim, shards_of):
        heights = jax.random.uniform(jax.random.fold_in(jax.random.fold_in(stream_key, 6), dim), (shards_of,), jnp.float32, least / len(shards), top_value / len(shards))
        return jnp.repeat(jnp.exp(heights), shape[dim] // shards_of).reshape((-1,) + (1,) * (len(shape) - dim - 1))

    gain = one(*shards[0])
    for cut in shards[1:]:
        gain = gain * one(*cut)
    return gain


def gaussian(key, shape, deviation, most, pieces=(), kind=jnp.bfloat16):
    factor_of = block_scale(key, shape, pieces, -0.22, 0.18) if pieces else 1.0
    entries = jax.random.normal(key, shape, jnp.float32) * deviation * factor_of
    return jnp.minimum(jnp.maximum(entries, -most), most).astype(kind)


def setup_inputs(seed: int = 0) -> dict:
    arg_keys = jax.random.split(jax.random.key(seed), 5)
    layer_deltas = gaussian(arg_keys[0], (LAYERS, TOKENS, D), 1.0, 6.0, ((0, 16), (1, 2), (2, 8)))
    tap_layers = draw_tap_layers(jax.random.fold_in(arg_keys[4], 71), 0)
    norm_gain = jnp.clip(1.0 + 0.18 * jax.random.normal(arg_keys[2], (TAPS, D), jnp.float32), 0.1, 1.9)
    fc_weight = gaussian(arg_keys[3], (TAPS, D, D), (3 * D) ** -0.5, 0.02734375, ((1, 8), (2, 32)))
    return {"layer_deltas": layer_deltas, "tap_layers": tap_layers, "norm_gain": norm_gain, "fc_weight": fc_weight}


EPS = 1e-05

def reference(layer_deltas, tap_layers, norm_gain, fc_weight):
    zeros = jnp.zeros((TOKENS, D), jnp.float32)
    start = jnp.zeros((TAPS, TOKENS, D), jnp.float32)

    def advance(carry, inputs):
        running, tapped = carry
        delta, index = inputs
        running = running + delta.astype(jnp.float32)
        hit = tap_layers == index
        tapped = jnp.where(hit[:, None, None], running[None], tapped)
        return ((running, tapped), None)
    layer_ids = jnp.arange(LAYERS, dtype=jnp.int32)
    (running, tapped), _ = lax.scan(advance, (zeros, start), (layer_deltas, layer_ids))
    squares = lax.optimization_barrier(jnp.mean(tapped * tapped, axis=2, keepdims=True))
    normed = (tapped * lax.rsqrt(squares + EPS) * norm_gain[:, None, :]).astype(jnp.bfloat16)
    joined = jnp.dot(normed[0], fc_weight[0], preferred_element_type=jnp.float32)
    joined = joined + jnp.dot(normed[1], fc_weight[1], preferred_element_type=jnp.float32)
    joined = joined + jnp.dot(normed[2], fc_weight[2], preferred_element_type=jnp.float32)
    return joined.astype(jnp.bfloat16)
```

```python
import jax
import jax.numpy as jnp
from jax import lax
from jax.experimental import pallas as pl
from jax.experimental.pallas import tpu as pltpu
from jax.sharding import Mesh, PartitionSpec as P

D = 16384
EPS = 1e-05
Z, CORE, HI, X, LO = "z", "core", "hi", "x", "lo"
BF, F32 = jnp.bfloat16, jnp.float32
ROWS = 16
HALF = 1024
MIB = 1 << 20

VMEM = pl.BlockSpec(memory_space=pltpu.VMEM)
SMEM = pl.BlockSpec(memory_space=pltpu.SMEM)


def call(kernel, shape, specs, *args, flops=0, limit=32):
    size = sum(a.size * a.dtype.itemsize for a in args)
    return pl.pallas_call(
        kernel,
        out_shape=shape,
        in_specs=specs,
        out_specs=VMEM,
        cost_estimate=pl.CostEstimate(flops=flops, bytes_accessed=size, transcendentals=0),
        compiler_params=pltpu.CompilerParams(vmem_limit_bytes=limit * MIB),
    )(*args)


def half_of(core):
    return pl.ds(pl.multiple_of(core * HALF, HALF), HALF)


def segments(tap_ref, delta_ref, tokens, columns):
    first = (lax.axis_index(Z) * 2 + lax.axis_index(CORE)) * 2
    layers = [delta_ref[j, tokens, columns].astype(F32) for j in range(2)]
    out = []
    for k in range(3):
        total = None
        for j in range(2):
            inside = first + j <= tap_ref[k]
            if k:
                inside = jnp.logical_and(inside, first + j > tap_ref[k - 1])
            term = layers[j] * jnp.where(inside, 1.0, 0.0).astype(F32)
            total = term if total is None else total + term
        out.append(total)
    return out


def send_kernel(tap_ref, delta_ref, out_ref):
    columns = half_of(1 - lax.axis_index(CORE))
    for piece in range(8):
        for k, part in enumerate(segments(tap_ref, delta_ref, pl.ds(piece * ROWS, ROWS), columns)):
            out_ref[piece, k] = part.astype(BF)


def pair_kernel(tap_ref, delta_ref, other_ref, out_ref):
    columns = half_of(lax.axis_index(CORE))
    for piece in range(8):
        for k, part in enumerate(segments(tap_ref, delta_ref, pl.ds(piece * ROWS, ROWS), columns)):
            out_ref[piece, k] = (part + other_ref[piece, k].astype(F32)).astype(BF)


def tapped_kernel(parts_ref, gain_ref, out_ref):
    columns = half_of(lax.axis_index(CORE))
    state = None
    for k in range(3):
        total = parts_ref[0, k].astype(F32)
        for piece in range(1, 8):
            total = total + parts_ref[piece, k].astype(F32)
        state = total if state is None else state + total
        scaled = (state * gain_ref[pl.ds(k, 1), columns]).astype(BF)
        for copy in range(out_ref.shape[0]):
            out_ref[copy, k] = scaled


def join_kernel(mine_ref, other_ref, weight_ref, gain_ref, out_ref):
    core = lax.axis_index(CORE)
    lane = lax.broadcasted_iota(jnp.int32, (16, 512), 1) // 64
    squares = [[None] * 3 for _ in range(16)]
    for k in range(3):
        total = None
        sums = None
        for ref, side in ((mine_ref, core), (other_ref, 1 - core)):
            states = ref[:, k].reshape(256, HALF)
            weights = weight_ref[k, half_of(side), :]
            product = jnp.dot(states, weights, preferred_element_type=F32)
            plain = states.astype(F32) / gain_ref[pl.ds(k, 1), half_of(side)]
            square = jnp.sum(plain * plain, axis=1, keepdims=True)
            total = product if total is None else total + product
            sums = square if sums is None else sums + square
        out_ref[:, k * 32 : (k + 1) * 32, :] = total.reshape(8, 32, 512).astype(BF)
        for block in range(16):
            squares[block][k] = sums[block * 16 : (block + 1) * 16]
    for piece in range(8):
        packed = jnp.zeros((16, 512), F32)
        for h in range(2):
            for k in range(3):
                packed = jnp.where(lane == 2 * k + h, squares[2 * piece + h][k], packed)
        out_ref[piece, 96:112, :] = packed.astype(BF)


def scale_kernel(parts_ref, out_ref):
    squares = parts_ref[0, 96:112, :].astype(F32)
    for piece in range(1, 8):
        squares = squares + parts_ref[piece, 96:112, :].astype(F32)
    scale = lax.rsqrt(squares / D + EPS)
    for h in range(2):
        joined = None
        for k in range(3):
            rows = pl.ds(k * 32 + h * 16, 16)
            total = parts_ref[0, rows, :].astype(F32)
            for piece in range(1, 8):
                total = total + parts_ref[piece, rows, :].astype(F32)
            at = 64 * (2 * k + h)
            total = total * scale[:, at : at + 1]
            joined = total if joined is None else joined + total
        joined = joined.astype(BF)
        for copy in range(8):
            out_ref[copy, h * 16 : (h + 1) * 16, :] = joined


def swap(a, axis):
    return lax.ppermute(a, axis, [(0, 1), (1, 0)])


def exchange(a, axes):
    return lax.all_to_all(a, axes, 0, 0, tiled=True)


def shards(layer_deltas, tap_layers, norm_gain, fc_weight):
    pieces = jax.ShapeDtypeStruct((8, 3, ROWS, HALF), BF)
    sent = call(send_kernel, pieces, [SMEM, VMEM], tap_layers, layer_deltas)
    other = swap(sent, CORE)
    paired = call(pair_kernel, pieces, [SMEM, VMEM, VMEM], tap_layers, layer_deltas, other)
    parts = exchange(paired, (Z,))
    copies = jax.ShapeDtypeStruct((16, 3, ROWS, HALF), BF)
    mine = call(tapped_kernel, copies, [VMEM, VMEM], parts, norm_gain)
    mine = exchange(mine, (LO, Z))
    other = swap(mine, CORE)
    partial = jax.ShapeDtypeStruct((8, 112, 512), BF)
    partial = call(
        join_kernel, partial, [VMEM] * 4, mine, other, fc_weight, norm_gain, flops=2 * 256 * 6144 * 512
    )
    partial = exchange(partial, (HI, X))
    joined = call(scale_kernel, jax.ShapeDtypeStruct((8, 32, 512), BF), [VMEM], partial)
    return exchange(joined, (HI, X)).reshape(256, 512)


def solution(mesh):
    fine = Mesh(mesh.devices.reshape(8, 2, 2, 4, 2), (Z, CORE, HI, X, LO))
    in_specs = (P((Z, CORE), LO, (HI, X)), P(), P(None, (HI, X)), P(None, (HI, X), (Z, CORE, LO)))
    out_specs = P(None, (Z, CORE, LO))
    return jax.shard_map(shards, mesh=fine, in_specs=in_specs, out_specs=out_specs, check_vma=False)
```

```python
import jax
import jax.numpy as jnp
from jax import lax
from jax.experimental import pallas as pl
from jax.experimental.pallas import tpu as pltpu
from jax.sharding import Mesh, PartitionSpec as P

D = 16384
EPS = 1e-05
ZQ, ZP, CORE, HI, X, LO = "zq", "zp", "core", "hi", "x", "lo"
Z = (ZQ, ZP)
BF, F32 = jnp.bfloat16, jnp.float32
ROWS = 16
HALF = 1024
MIB = 1 << 20

VMEM = pl.BlockSpec(memory_space=pltpu.VMEM)
SMEM = pl.BlockSpec(memory_space=pltpu.SMEM)
HBM = pl.BlockSpec(memory_space=pltpu.HBM)


def call(kernel, shapes, specs, *args, flops=0, limit=24, scratch=()):
    size = sum(a.size * a.dtype.itemsize for a in args)
    single = not isinstance(shapes, list)
    shapes = [shapes] if single else shapes
    out = pl.pallas_call(
        kernel,
        out_shape=[space(shape, kind) for shape, kind, space in shapes],
        in_specs=specs,
        out_specs=[pl.BlockSpec(memory_space=space) for _, _, space in shapes],
        scratch_shapes=list(scratch),
        cost_estimate=pl.CostEstimate(flops=flops, bytes_accessed=size, transcendentals=0),
        compiler_params=pltpu.CompilerParams(vmem_limit_bytes=limit * MIB),
    )(*args)
    return out[0] if single else out


def half_of(core):
    return pl.ds(pl.multiple_of(core * HALF, HALF), HALF)


def segments(tap_ref, delta_ref, tokens, columns):
    section = lax.axis_index(ZQ) * 4 + lax.axis_index(ZP) * 2 + lax.axis_index(CORE)
    first = section * 2
    layers = [delta_ref[j, tokens, columns].astype(F32) for j in range(2)]
    out = []
    for k in range(3):
        total = None
        for j in range(2):
            inside = first + j <= tap_ref[k]
            if k:
                inside = jnp.logical_and(inside, first + j > tap_ref[k - 1])
            term = layers[j] * jnp.where(inside, 1.0, 0.0).astype(F32)
            total = term if total is None else total + term
        out.append(total)
    return out


def send_kernel(tap_hbm, delta_hbm, gain_hbm, out_ref, tap_ref, delta_ref, gain_ref, sems):
    columns = half_of(1 - lax.axis_index(CORE))
    pairs = ((tap_hbm, tap_ref), (delta_hbm, delta_ref), (gain_hbm, gain_ref))
    copies = [pltpu.make_async_copy(a, b, sems.at[i]) for i, (a, b) in enumerate(pairs)]
    for copy in copies:
        copy.start()
    for copy in copies:
        copy.wait()
    for piece in range(8):
        for k, part in enumerate(segments(tap_ref, delta_ref, pl.ds(piece * ROWS, ROWS), columns)):
            out_ref[piece, k] = part.astype(BF)


def pair_kernel(tap_ref, delta_ref, other_ref, out_ref):
    columns = half_of(lax.axis_index(CORE))
    for piece in range(8):
        for k, part in enumerate(segments(tap_ref, delta_ref, pl.ds(piece * ROWS, ROWS), columns)):
            out_ref[piece, k] = (part + other_ref[piece, k].astype(F32)).astype(BF)


def tapped_kernel(parts_ref, gain_ref, out_ref):
    columns = half_of(lax.axis_index(CORE))
    state = None
    for k in range(3):
        total = parts_ref[0, k].astype(F32)
        for piece in range(1, 8):
            total = total + parts_ref[piece, k].astype(F32)
        state = total if state is None else state + total
        scaled = (state * gain_ref[pl.ds(k, 1), columns]).astype(BF)
        for copy in range(out_ref.shape[0]):
            out_ref[copy, k] = scaled


def blocks_of():
    zq, zp, lo = lax.axis_index(ZQ), lax.axis_index(ZP), lax.axis_index(LO)
    half = lax.rem(zq, 2)
    left = lax.rem(zq + zp + 1, 2)
    mine, yours, here, there = lo * 8, 8 - lo * 8, zp, 1 - zp
    out = [mine + 2 * i + here for i in range(4)]
    out += [mine + 2 * i + there for i in range(4)]
    out += [yours + 2 * (2 * half + i) + here for i in range(2)]
    out += [yours + 2 * (2 * left + i) + there for i in range(2)]
    out += [yours + 2 * (2 - 2 * left + i) + there for i in range(2)]
    out += [yours + 2 * (2 - 2 * half + i) + here for i in range(2)]
    return out


def cut_kernel(same_ref, left_ref, right_ref, early_ref, late_ref):
    at = 2 * lax.rem(lax.axis_index(ZQ), 2)
    left_ref[...] = same_ref[:2]
    right_ref[...] = same_ref[2:]
    early_ref[...] = same_ref[pl.ds(at, 2)]
    late_ref[...] = same_ref[pl.ds(2 - at, 2)]


def pack_kernel(*refs):
    for i, ref in enumerate(refs[:-1]):
        refs[-1][2 * i : 2 * i + 2] = ref[...]


def join_kernel(*refs):
    mine_refs, other_refs, (weight_ref, gain_ref, out_ref, state_ref) = refs[:3], refs[3:6], refs[6:]
    core = lax.axis_index(CORE)
    blocks = blocks_of()
    lane = lax.broadcasted_iota(jnp.int32, (16, 512), 1) // 64
    squares = [[None] * 3 for _ in range(16)]
    for k in range(3):
        total = None
        sums = None
        for side_refs, side in ((mine_refs, core), (other_refs, 1 - core)):
            at = 0
            for ref in side_refs:
                rows = ref.shape[0] * ROWS
                state_ref[at : at + rows, :] = ref[:, k].reshape(rows, HALF)
                at += rows
            states = state_ref[...]
            weights = weight_ref[k, half_of(side), :]
            product = jnp.dot(states, weights, preferred_element_type=F32)
            plain = states.astype(F32) / gain_ref[pl.ds(k, 1), half_of(side)]
            square = jnp.sum(plain * plain, axis=1, keepdims=True)
            total = product if total is None else total + product
            sums = square if sums is None else sums + square
        total = total.astype(BF)
        for i in range(16):
            rows = slice(i * ROWS, (i + 1) * ROWS)
            at = pl.multiple_of(k * 32 + lax.rem(blocks[i], 2) * 16, 16)
            out_ref[blocks[i] // 2, pl.ds(at, 16), :] = total[rows]
            squares[i][k] = sums[rows]
    out_ref[:, 96:112, :] = jnp.zeros((8, 16, 512), BF)
    for i in range(16):
        packed = out_ref[blocks[i] // 2, 96:112, :].astype(F32)
        for k in range(3):
            packed = jnp.where(lane == 2 * k + lax.rem(blocks[i], 2), squares[i][k], packed)
        out_ref[blocks[i] // 2, 96:112, :] = packed.astype(BF)


def scale_kernel(parts_ref, out_ref):
    squares = parts_ref[0, 96:112, :].astype(F32)
    for piece in range(1, 8):
        squares = squares + parts_ref[piece, 96:112, :].astype(F32)
    scale = lax.rsqrt(squares / D + EPS)
    for h in range(2):
        joined = None
        for k in range(3):
            rows = pl.ds(k * 32 + h * 16, 16)
            total = parts_ref[0, rows, :].astype(F32)
            for piece in range(1, 8):
                total = total + parts_ref[piece, rows, :].astype(F32)
            at = 64 * (2 * k + h)
            total = total * scale[:, at : at + 1]
            joined = total if joined is None else joined + total
        joined = joined.astype(BF)
        for copy in range(8):
            out_ref[copy, h * 16 : (h + 1) * 16, :] = joined


def swap(a, axis):
    return lax.ppermute(a, axis, [(0, 1), (1, 0)])


def along(a, step):
    return lax.ppermute(a, Z, [(i, (i + step) % 8) for i in range(8)])


def exchange(a, axes):
    return lax.all_to_all(a, axes, 0, 0, tiled=True)


def gather(mine):
    two = ((2, 3, ROWS, HALF), BF, pltpu.VMEM)
    six = ((6, 3, ROWS, HALF), BF, pltpu.VMEM)
    same = exchange(mine, ZQ)
    left, right, early, late = call(cut_kernel, [two] * 4, [VMEM], same)
    same_other = swap(same, CORE)
    left, right, early = along(left, 1), along(right, -1), swap(early, LO)
    left, right, early, late = lax.optimization_barrier((left, right, early, late))
    early_left, early_right, late = along(early, 1), along(early, -1), swap(late, LO)
    middle = call(pack_kernel, six, [VMEM] * 3, left, right, early)
    middle_other = swap(middle, CORE)
    last = call(pack_kernel, six, [VMEM] * 3, early_left, early_right, late)
    return same, middle, last, same_other, middle_other, swap(last, CORE)


def shards(layer_deltas, tap_layers, norm_gain, fc_weight):
    pieces = ((8, 3, ROWS, HALF), BF, pltpu.VMEM)
    sources = [pltpu.with_memory_space_constraint(a, pltpu.HBM) for a in (tap_layers, layer_deltas, norm_gain)]
    sent, taps, deltas, gain = call(
        send_kernel,
        [
            pieces,
            (tap_layers.shape, jnp.int32, pltpu.SMEM),
            (layer_deltas.shape, BF, pltpu.VMEM),
            (norm_gain.shape, F32, pltpu.VMEM),
        ],
        [HBM] * 3,
        *sources,
        scratch=[pltpu.SemaphoreType.DMA((3,))],
    )
    other = swap(sent, CORE)
    paired = call(pair_kernel, pieces, [SMEM, VMEM, VMEM], taps, deltas, other)
    parts = exchange(paired, Z)
    mine = call(tapped_kernel, ((4, 3, ROWS, HALF), BF, pltpu.VMEM), [VMEM, VMEM], parts, gain)
    states = gather(mine)
    partial = call(
        join_kernel,
        ((8, 112, 512), BF, pltpu.VMEM),
        [VMEM] * 8,
        *states,
        fc_weight,
        gain,
        flops=2 * 256 * 6144 * 512,
        scratch=[pltpu.VMEM((256, HALF), BF)],
    )
    partial = exchange(partial, (HI, X))
    joined = call(scale_kernel, ((8, 32, 512), BF, pltpu.VMEM), [VMEM], partial)
    return exchange(joined, (HI, X)).reshape(256, 512)


def solution(mesh):
    fine = Mesh(mesh.devices.reshape(4, 2, 2, 2, 4, 2), (ZQ, ZP, CORE, HI, X, LO))
    section, tensor = (ZQ, ZP, CORE), (HI, X)
    in_specs = (P(section, LO, tensor), P(), P(None, tensor), P(None, tensor, (*section, LO)))
    out_specs = P(None, (*section, LO))
    return jax.shard_map(shards, mesh=fine, in_specs=in_specs, out_specs=out_specs, check_vma=False)
```

```python
import jax
import jax.numpy as jnp
from jax import lax
from jax.experimental import pallas as pl
from jax.experimental.pallas import tpu as pltpu
from jax.sharding import Mesh, PartitionSpec as P

D = 16384
EPS = 1e-05
ZQ, ZP, CORE, HI, X, LO = "zq", "zp", "core", "hi", "x", "lo"
Z = (ZQ, ZP)
BF, F32 = jnp.bfloat16, jnp.float32
ROWS = 16
HALF = 1024
MIB = 1 << 20

VMEM = pl.BlockSpec(memory_space=pltpu.VMEM)
SMEM = pl.BlockSpec(memory_space=pltpu.SMEM)
HBM = pl.BlockSpec(memory_space=pltpu.HBM)
ANY = pl.BlockSpec(memory_space=pl.ANY)


def call(kernel, shapes, specs, *args, flops=0, limit=24, scratch=()):
    size = sum(a.size * a.dtype.itemsize for a in args)
    single = not isinstance(shapes, list)
    shapes = [shapes] if single else shapes
    out = pl.pallas_call(
        kernel,
        out_shape=[space(shape, kind) for shape, kind, space in shapes],
        in_specs=specs,
        out_specs=[pl.BlockSpec(memory_space=space) for _, _, space in shapes],
        scratch_shapes=list(scratch),
        cost_estimate=pl.CostEstimate(flops=flops, bytes_accessed=size, transcendentals=0),
        compiler_params=pltpu.CompilerParams(vmem_limit_bytes=limit * MIB),
    )(*args)
    return out[0] if single else out


def half_of(core):
    return pl.ds(pl.multiple_of(core * HALF, HALF), HALF)


def segment(layer, tap_ref):
    return (layer > tap_ref[0]).astype(jnp.int32) + (layer > tap_ref[1]).astype(jnp.int32)


def load_kernel(tap_hbm, delta_hbm, gain_hbm, other_ref, mine_ref, tap_ref, gain_ref, three_ref, sems):
    core = lax.axis_index(CORE)
    pairs = (
        (delta_hbm.at[:, :, half_of(1 - core)], other_ref),
        (delta_hbm.at[:, :, half_of(core)], mine_ref),
        (tap_hbm, tap_ref),
        (gain_hbm, gain_ref),
    )
    copies = [pltpu.make_async_copy(a, b, sems.at[i]) for i, (a, b) in enumerate(pairs)]
    for copy in copies:
        copy.start()
    for copy in copies:
        copy.wait()
    three_ref[0] = (tap_ref[0] // 4 == tap_ref[1] // 4).astype(jnp.int32)


def pair_kernel(tap_ref, mine_ref, other_ref, ends_ref, middle_ref):
    core = lax.axis_index(CORE)
    first = (lax.axis_index(ZQ) * 2 + lax.axis_index(ZP)) * 4
    head, tail = segment(first, tap_ref), segment(first + 3, tap_ref)
    weights = []
    for side in (core, 1 - core):
        for j in range(2):
            at = segment(first + 2 * side + j, tap_ref)
            in_head = at == head
            in_tail = jnp.logical_and(at == tail, tail != head)
            between = jnp.logical_not(jnp.logical_or(in_head, in_tail))
            weights.append([jnp.where(w, 1.0, 0.0).astype(F32) for w in (in_head, in_tail, between)])
    for piece in range(8):
        rows = slice(piece * ROWS, (piece + 1) * ROWS)
        layers = [ref[j, rows].astype(F32) for ref in (mine_ref, other_ref) for j in range(2)]
        sums = []
        for part in range(3):
            terms = [layer * weight[part] for layer, weight in zip(layers, weights)]
            sums.append(((terms[0] + terms[1]) + (terms[2] + terms[3])).astype(BF))
        ends_ref[piece, 0] = sums[0]
        ends_ref[piece, 1] = sums[1]
        middle_ref[piece] = sums[2]


def tapped_kernel(tap_ref, ends_ref, middle_ref, gain_ref, out_ref):
    columns = half_of(lax.axis_index(CORE))
    between = middle_ref[0].astype(F32)
    for chip in range(1, 8):
        between = between + middle_ref[chip].astype(F32)
    for k in range(3):
        state = between if k else jnp.zeros_like(between)
        for chip in range(8):
            for end in range(2):
                inside = jnp.where(4 * chip + 3 * end <= tap_ref[k], 1.0, 0.0).astype(F32)
                state = state + ends_ref[chip, end].astype(F32) * inside
        scaled = (state * gain_ref[pl.ds(k, 1), columns]).astype(BF)
        for copy in range(out_ref.shape[0]):
            out_ref[copy, k] = scaled


def blocks_of():
    zq, zp, lo = lax.axis_index(ZQ), lax.axis_index(ZP), lax.axis_index(LO)
    half = lax.rem(zq, 2)
    left = lax.rem(zq + zp + 1, 2)
    mine, yours, here, there = lo * 8, 8 - lo * 8, zp, 1 - zp
    out = [mine + 2 * i + here for i in range(4)]
    out += [mine + 2 * i + there for i in range(4)]
    out += [yours + 2 * (2 * half + i) + here for i in range(2)]
    out += [yours + 2 * (2 * left + i) + there for i in range(2)]
    out += [yours + 2 * (2 - 2 * left + i) + there for i in range(2)]
    out += [yours + 2 * (2 - 2 * half + i) + here for i in range(2)]
    return out


def cut_kernel(same_ref, left_ref, right_ref, early_ref, late_ref):
    at = 2 * lax.rem(lax.axis_index(ZQ), 2)
    left_ref[...] = same_ref[:2]
    right_ref[...] = same_ref[2:]
    early_ref[...] = same_ref[pl.ds(at, 2)]
    late_ref[...] = same_ref[pl.ds(2 - at, 2)]


def pack_kernel(*refs):
    for i, ref in enumerate(refs[:3]):
        refs[-1][2 * i : 2 * i + 2] = ref[...]


def fetch_kernel(weight_hbm, after_ref, weight_ref, sem):
    del after_ref
    copy = pltpu.make_async_copy(weight_hbm, weight_ref, sem)
    copy.start()
    copy.wait()


def join_kernel(*refs):
    mine_refs, other_refs, (weight_ref, gain_ref, out_ref, state_ref) = refs[:3], refs[3:6], refs[6:]
    core = lax.axis_index(CORE)
    blocks = blocks_of()
    lane = lax.broadcasted_iota(jnp.int32, (16, 512), 1) // 64
    squares = [[None] * 3 for _ in range(16)]
    for k in range(3):
        total = None
        sums = None
        for side_refs, side in ((mine_refs, core), (other_refs, 1 - core)):
            at = 0
            for ref in side_refs:
                rows = ref.shape[0] * ROWS
                state_ref[at : at + rows, :] = ref[:, k].reshape(rows, HALF)
                at += rows
            states = state_ref[...]
            weights = weight_ref[k, half_of(side), :]
            product = jnp.dot(states, weights, preferred_element_type=F32)
            plain = states.astype(F32) / gain_ref[pl.ds(k, 1), half_of(side)]
            square = jnp.sum(plain * plain, axis=1, keepdims=True)
            total = product if total is None else total + product
            sums = square if sums is None else sums + square
        total = total.astype(BF)
        for i in range(16):
            rows = slice(i * ROWS, (i + 1) * ROWS)
            at = pl.multiple_of(k * 32 + lax.rem(blocks[i], 2) * 16, 16)
            out_ref[blocks[i] // 2, pl.ds(at, 16), :] = total[rows]
            squares[i][k] = sums[rows]
    out_ref[:, 96:112, :] = jnp.zeros((8, 16, 512), BF)
    for i in range(16):
        packed = out_ref[blocks[i] // 2, 96:112, :].astype(F32)
        for k in range(3):
            packed = jnp.where(lane == 2 * k + lax.rem(blocks[i], 2), squares[i][k], packed)
        out_ref[blocks[i] // 2, 96:112, :] = packed.astype(BF)


def scale_kernel(parts_ref, out_ref):
    squares = parts_ref[0, 96:112, :].astype(F32)
    for piece in range(1, 8):
        squares = squares + parts_ref[piece, 96:112, :].astype(F32)
    scale = lax.rsqrt(squares / D + EPS)
    for h in range(2):
        joined = None
        for k in range(3):
            rows = pl.ds(k * 32 + h * 16, 16)
            total = parts_ref[0, rows, :].astype(F32)
            for piece in range(1, 8):
                total = total + parts_ref[piece, rows, :].astype(F32)
            at = 64 * (2 * k + h)
            total = total * scale[:, at : at + 1]
            joined = total if joined is None else joined + total
        joined = joined.astype(BF)
        for copy in range(8):
            out_ref[copy, h * 16 : (h + 1) * 16, :] = joined


def swap(a, axis):
    return lax.ppermute(a, axis, [(0, 1), (1, 0)])


def along(a, step):
    return lax.ppermute(a, Z, [(i, (i + step) % 8) for i in range(8)])


def exchange(a, axes):
    return lax.all_to_all(a, axes, 0, 0, tiled=True)


def gather(mine, weight):
    two = ((2, 3, ROWS, HALF), BF, pltpu.VMEM)
    six = ((6, 3, ROWS, HALF), BF, pltpu.VMEM)
    same = exchange(mine, ZQ)
    left, right, early, late = call(cut_kernel, [two] * 4, [VMEM], same)
    same_other = swap(same, CORE)
    left, right, early = along(left, 1), along(right, -1), swap(early, LO)
    left, right, early, late = lax.optimization_barrier((left, right, early, late))
    early_left, early_right, late = along(early, 1), along(early, -1), swap(late, LO)
    middle = call(pack_kernel, six, [VMEM] * 3, left, right, early)
    middle_other = swap(middle, CORE)
    weight = call(
        fetch_kernel,
        (weight.shape, BF, pltpu.VMEM),
        [HBM, ANY],
        pltpu.with_memory_space_constraint(weight, pltpu.HBM),
        middle,
        scratch=[pltpu.SemaphoreType.DMA],
    )
    last = call(pack_kernel, six, [VMEM] * 3 + [ANY], early_left, early_right, late, weight)
    return same, middle, last, same_other, middle_other, swap(last, CORE), weight


def shards(layer_deltas, tap_layers, norm_gain, fc_weight):
    raw = ((2, 128, HALF), BF, pltpu.VMEM)
    sources = [pltpu.with_memory_space_constraint(a, pltpu.HBM) for a in (tap_layers, layer_deltas, norm_gain)]
    sent, own, taps, gain, three = call(
        load_kernel,
        [
            raw,
            raw,
            (tap_layers.shape, jnp.int32, pltpu.SMEM),
            (norm_gain.shape, F32, pltpu.VMEM),
            ((1,), jnp.int32, pltpu.SMEM),
        ],
        [HBM] * 3,
        *sources,
        scratch=[pltpu.SemaphoreType.DMA((4,))],
    )
    ends, middle = call(
        pair_kernel,
        [((8, 2, ROWS, HALF), BF, pltpu.VMEM), ((8, ROWS, HALF), BF, pltpu.VMEM)],
        [SMEM, VMEM, VMEM],
        taps,
        own,
        swap(sent, CORE),
    )
    ends = exchange(ends, Z)
    middle = lax.cond(three[0] != 0, lambda a: exchange(a, Z), lambda a: a, middle)
    mine = call(
        tapped_kernel,
        ((4, 3, ROWS, HALF), BF, pltpu.VMEM),
        [SMEM, VMEM, VMEM, VMEM],
        taps,
        ends,
        middle,
        gain,
    )
    states = gather(mine, fc_weight)
    partial = call(
        join_kernel,
        ((8, 112, 512), BF, pltpu.VMEM),
        [VMEM] * 8,
        *states,
        gain,
        flops=2 * 256 * 6144 * 512,
        scratch=[pltpu.VMEM((256, HALF), BF)],
    )
    partial = exchange(partial, (HI, X))
    joined = call(scale_kernel, ((8, 32, 512), BF, pltpu.VMEM), [VMEM], partial)
    return exchange(joined, (HI, X)).reshape(256, 512)


def solution(mesh):
    fine = Mesh(mesh.devices.reshape(4, 2, 2, 2, 4, 2), (ZQ, ZP, CORE, HI, X, LO))
    section, tensor = (ZQ, ZP, CORE), (HI, X)
    in_specs = (P(section, LO, tensor), P(), P(None, tensor), P(None, tensor, (*section, LO)))
    out_specs = P(None, (*section, LO))
    return jax.shard_map(shards, mesh=fine, in_specs=in_specs, out_specs=out_specs, check_vma=False)
```

```python
import functools

import jax
import jax.numpy as jnp
from jax import lax
from jax.experimental import pallas as pl
from jax.experimental.pallas import tpu as pltpu
from jax.sharding import Mesh, PartitionSpec as P

D = 16384
EPS = 1e-05
ZQ, ZP, CORE, HI, X, LO = "zq", "zp", "core", "hi", "x", "lo"
Z = (ZQ, ZP)
BF, F32 = jnp.bfloat16, jnp.float32
ROWS = 16
HALF = 1024
MIB = 1 << 20

VMEM = pl.BlockSpec(memory_space=pltpu.VMEM)
SMEM = pl.BlockSpec(memory_space=pltpu.SMEM)
HBM = pl.BlockSpec(memory_space=pltpu.HBM)
ANY = pl.BlockSpec(memory_space=pl.ANY)


def call(kernel, shapes, specs, *args, flops=0, limit=24, scratch=(), alias=None):
    size = sum(a.size * a.dtype.itemsize for a in args)
    single = not isinstance(shapes, list)
    shapes = [shapes] if single else shapes
    out = pl.pallas_call(
        kernel,
        out_shape=[space(shape, kind) for shape, kind, space in shapes],
        in_specs=specs,
        out_specs=[pl.BlockSpec(memory_space=space) for _, _, space in shapes],
        scratch_shapes=list(scratch),
        input_output_aliases=alias or {},
        cost_estimate=pl.CostEstimate(flops=flops, bytes_accessed=size, transcendentals=0),
        compiler_params=pltpu.CompilerParams(vmem_limit_bytes=limit * MIB),
    )(*args)
    return out[0] if single else out


def half_of(core):
    return pl.ds(pl.multiple_of(core * HALF, HALF), HALF)


def segment(layer, tap_ref):
    return (layer > tap_ref[0]).astype(jnp.int32) + (layer > tap_ref[1]).astype(jnp.int32)


def load_kernel(tap_hbm, delta_hbm, gain_hbm, other_ref, mine_ref, tap_ref, gain_ref, three_ref, sems):
    core = lax.axis_index(CORE)
    pairs = (
        (delta_hbm.at[:, :, half_of(1 - core)], other_ref),
        (delta_hbm.at[:, :, half_of(core)], mine_ref),
        (tap_hbm, tap_ref),
        (gain_hbm, gain_ref),
    )
    copies = [pltpu.make_async_copy(a, b, sems.at[i]) for i, (a, b) in enumerate(pairs)]
    for copy in copies:
        copy.start()
    for copy in copies:
        copy.wait()
    three_ref[0] = (tap_ref[0] // 4 == tap_ref[1] // 4).astype(jnp.int32)


def pair_kernel(tap_ref, mine_ref, other_ref, ends_ref, middle_ref):
    core = lax.axis_index(CORE)
    first = (lax.axis_index(ZQ) * 2 + lax.axis_index(ZP)) * 4
    head, tail = segment(first, tap_ref), segment(first + 3, tap_ref)
    weights = []
    for side in (core, 1 - core):
        for j in range(2):
            at = segment(first + 2 * side + j, tap_ref)
            in_head = at == head
            in_tail = jnp.logical_and(at == tail, tail != head)
            between = jnp.logical_not(jnp.logical_or(in_head, in_tail))
            weights.append([jnp.where(w, 1.0, 0.0).astype(F32) for w in (in_head, in_tail, between)])
    for piece in range(8):
        rows = slice(piece * ROWS, (piece + 1) * ROWS)
        layers = [ref[j, rows].astype(F32) for ref in (mine_ref, other_ref) for j in range(2)]
        sums = []
        for part in range(3):
            terms = [layer * weight[part] for layer, weight in zip(layers, weights)]
            sums.append(((terms[0] + terms[1]) + (terms[2] + terms[3])).astype(BF))
        ends_ref[piece, 0] = sums[0]
        ends_ref[piece, 1] = sums[1]
        middle_ref[piece] = sums[2]


def tapped_kernel(tap_ref, ends_ref, middle_ref, gain_ref, out_ref):
    columns = half_of(lax.axis_index(CORE))
    between = middle_ref[0].astype(F32)
    for chip in range(1, 8):
        between = between + middle_ref[chip].astype(F32)
    for k in range(3):
        state = between if k else jnp.zeros_like(between)
        for chip in range(8):
            for end in range(2):
                inside = jnp.where(4 * chip + 3 * end <= tap_ref[k], 1.0, 0.0).astype(F32)
                state = state + ends_ref[chip, end].astype(F32) * inside
        out_ref[0, k] = (state * gain_ref[pl.ds(k, 1), columns]).astype(BF)


def blocks_of():
    z = 2 * lax.axis_index(ZQ) + lax.axis_index(ZP)
    mine = lax.axis_index(LO) * 8
    yours = 8 - mine
    early = [mine + lax.rem(z + step, 8) for step in (0, 6, 2, 4)] + [yours + z]
    early += [mine + lax.rem(z + 7, 8), mine + lax.rem(z + 5, 8), yours + lax.rem(z + 7, 8)]
    early += [mine + lax.rem(z + 1, 8), mine + lax.rem(z + 3, 8), yours + lax.rem(z + 1, 8)]
    early += [yours + lax.rem(z + step, 8) for step in (2, 6, 4)]
    return early, [yours + lax.rem(z + 5, 8), yours + lax.rem(z + 3, 8)]


def cut_kernel(piece, below, above, far, near, right_ref, left_ref, across_ref, head_ref, tail_ref):
    for out_ref, refs in (
        (right_ref, (piece, below, near)),
        (left_ref, (piece, above, near)),
        (across_ref, (above, below, far)),
        (head_ref, (piece, below)),
        (tail_ref, (above, far)),
    ):
        for i, ref in enumerate(refs):
            out_ref[i] = ref[0]


def pack_kernel(count, *refs):
    out_ref = refs[-1]
    at = 0
    for ref in refs[:count]:
        out_ref[at : at + ref.shape[0]] = ref[...]
        at += ref.shape[0]


def ends_kernel(across_ref, left_ref, right_ref):
    left_ref[0] = across_ref[0]
    right_ref[0] = across_ref[1]


def fetch_kernel(weight_hbm, after_ref, weight_ref, sem):
    del after_ref
    copy = pltpu.make_async_copy(weight_hbm, weight_ref, sem)
    copy.start()
    copy.wait()


def join(blocks, sides, weight_ref, gain_ref, out_ref, state_ref):
    lane = lax.broadcasted_iota(jnp.int32, (ROWS, 128), 1) // ROWS
    squares = [[None] * 3 for _ in blocks]
    for k in range(3):
        total = None
        sums = None
        for refs, side in sides:
            at = 0
            for ref in refs:
                rows = ref.shape[0] * ROWS
                state_ref[at : at + rows, :] = ref[:, k].reshape(rows, HALF)
                at += rows
            states = state_ref[...]
            product = jnp.dot(states, weight_ref[k, half_of(side), :], preferred_element_type=F32)
            plain = states.astype(F32) * (1.0 / gain_ref[pl.ds(k, 1), half_of(side)])
            square = jnp.sum(plain * plain, axis=1, keepdims=True)
            total = product if total is None else total + product
            sums = square if sums is None else sums + square
        total = total.astype(BF)
        for i, block in enumerate(blocks):
            rows = slice(i * ROWS, (i + 1) * ROWS)
            squares[i][k] = sums[rows]
            for column in range(4):
                at = pl.multiple_of((k * 4 + column) * 32 + lax.rem(block, 2) * ROWS, ROWS)
                out_ref[block // 2, pl.ds(at, ROWS), :] = total[rows, column * 128 : (column + 1) * 128]
    for i, block in enumerate(blocks):
        packed = out_ref[block // 2, 384:400, :].astype(F32)
        for k in range(3):
            packed = jnp.where(lane == 2 * k + lax.rem(block, 2), squares[i][k], packed)
        out_ref[block // 2, 384:400, :] = packed.astype(BF)


def early_kernel(head, middle, head_other, middle_other, weight_ref, gain_ref, out_ref, state_ref):
    core = lax.axis_index(CORE)
    out_ref[:, 384:400, :] = jnp.zeros((8, ROWS, 128), BF)
    sides = (((head, middle), core), ((head_other, middle_other), 1 - core))
    join(blocks_of()[0], sides, weight_ref, gain_ref, out_ref, state_ref)


def last_kernel(early_ref, last, last_other, weight_ref, gain_ref, out_ref, state_ref):
    del early_ref
    core = lax.axis_index(CORE)
    join(blocks_of()[1], (((last,), core), ((last_other,), 1 - core)), weight_ref, gain_ref, out_ref, state_ref)


def scale_kernel(parts_ref, out_ref):
    squares = parts_ref[0, 384:400, :].astype(F32)
    for piece in range(1, 8):
        squares = squares + parts_ref[piece, 384:400, :].astype(F32)
    scale = lax.rsqrt(squares / D + EPS)
    for h in range(2):
        for column in range(4):
            joined = None
            for k in range(3):
                rows = pl.ds((k * 4 + column) * 32 + h * ROWS, ROWS)
                total = parts_ref[0, rows, :].astype(F32)
                for piece in range(1, 8):
                    total = total + parts_ref[piece, rows, :].astype(F32)
                at = ROWS * (2 * k + h)
                total = total * scale[:, at : at + 1]
                joined = total if joined is None else joined + total
            joined = joined.astype(BF)
            for copy in range(8):
                out_ref[copy, h * ROWS : (h + 1) * ROWS, column * 128 : (column + 1) * 128] = joined


def swap(a, axis):
    return lax.ppermute(a, axis, [(0, 1), (1, 0)])


def along(a, step):
    return lax.ppermute(a, Z, [(i, (i + step) % 8) for i in range(8)])


def exchange(a, axes):
    return lax.all_to_all(a, axes, 0, 0, tiled=True)


def states(count):
    return ((count, 3, ROWS, HALF), BF, pltpu.VMEM)


def shards(layer_deltas, tap_layers, norm_gain, fc_weight):
    raw = ((2, 128, HALF), BF, pltpu.VMEM)
    sources = [pltpu.with_memory_space_constraint(a, pltpu.HBM) for a in (tap_layers, layer_deltas, norm_gain)]
    sent, own, taps, gain, three = call(
        load_kernel,
        [
            raw,
            raw,
            (tap_layers.shape, jnp.int32, pltpu.SMEM),
            (norm_gain.shape, F32, pltpu.VMEM),
            ((1,), jnp.int32, pltpu.SMEM),
        ],
        [HBM] * 3,
        *sources,
        scratch=[pltpu.SemaphoreType.DMA((4,))],
    )
    ends, middle = call(
        pair_kernel,
        [((8, 2, ROWS, HALF), BF, pltpu.VMEM), ((8, ROWS, HALF), BF, pltpu.VMEM)],
        [SMEM, VMEM, VMEM],
        taps,
        own,
        swap(sent, CORE),
    )
    ends = exchange(ends, Z)
    middle = lax.cond(three[0] != 0, lambda a: exchange(a, Z), lambda a: a, middle)
    piece = call(tapped_kernel, states(1), [SMEM, VMEM, VMEM, VMEM], taps, ends, middle, gain)
    far = along(piece, 4)
    below, above = along(piece, 2), along(piece, -2)
    near = swap(piece, LO)
    parts = [states(3)] * 3 + [states(2)] * 2
    right, left, across, head, tail = call(cut_kernel, parts, [VMEM] * 5, piece, below, above, far, near)
    weight = call(
        fetch_kernel,
        (fc_weight.shape, BF, pltpu.VMEM),
        [HBM, ANY],
        pltpu.with_memory_space_constraint(fc_weight, pltpu.HBM),
        across,
        scratch=[pltpu.SemaphoreType.DMA],
    )
    first = (along(right, 1), along(left, -1), swap(across, LO), swap(head, CORE), weight)
    from_left, from_right, across, head_other, weight = lax.optimization_barrier(first)
    left, right = call(ends_kernel, [states(1)] * 2, [VMEM], across)
    far_left, far_right = along(right, 1), along(left, -1)
    pack = functools.partial(pack_kernel, 5)
    middle = call(pack, states(12), [VMEM] * 5, tail, near, from_left, from_right, across)
    payload = ((8, 400, 128), BF, pltpu.VMEM)
    partial = call(
        early_kernel,
        payload,
        [VMEM] * 6,
        head,
        middle,
        head_other,
        swap(middle, CORE),
        weight,
        gain,
        flops=2 * 224 * 6144 * 512,
        scratch=[pltpu.VMEM((224, HALF), BF)],
    )
    pack = functools.partial(pack_kernel, 2)
    last = call(pack, states(2), [VMEM, VMEM, ANY], far_left, far_right, partial)
    partial = call(
        last_kernel,
        payload,
        [VMEM] * 5,
        partial,
        last,
        swap(last, CORE),
        weight,
        gain,
        flops=2 * 32 * 6144 * 512,
        scratch=[pltpu.VMEM((32, HALF), BF)],
        alias={0: 0},
    )
    partial = exchange(partial, (HI, X))
    joined = call(scale_kernel, ((8, 32, 512), BF, pltpu.VMEM), [VMEM], partial)
    return exchange(joined, (HI, X)).reshape(256, 512)


def solution(mesh):
    fine = Mesh(mesh.devices.reshape(4, 2, 2, 2, 4, 2), (ZQ, ZP, CORE, HI, X, LO))
    section, tensor = (ZQ, ZP, CORE), (HI, X)
    in_specs = (P(section, LO, tensor), P(), P(None, tensor), P(None, tensor, (*section, LO)))
    out_specs = P(None, (*section, LO))
    return jax.shard_map(shards, mesh=fine, in_specs=in_specs, out_specs=out_specs, check_vma=False)
```

```python
import functools

import jax
import jax.numpy as jnp
from jax import lax
from jax.experimental import pallas as pl
from jax.experimental.pallas import tpu as pltpu
from jax.sharding import Mesh, PartitionSpec as P

D = 16384
EPS = 1e-05
ZQ, ZP, CORE, HI, X, LO = "zq", "zp", "core", "hi", "x", "lo"
Z = (ZQ, ZP)
BF, F32 = jnp.bfloat16, jnp.float32
ROWS = 16
HALF = 1024
MIB = 1 << 20

VMEM = pl.BlockSpec(memory_space=pltpu.VMEM)
SMEM = pl.BlockSpec(memory_space=pltpu.SMEM)
HBM = pl.BlockSpec(memory_space=pltpu.HBM)
ANY = pl.BlockSpec(memory_space=pl.ANY)


def call(kernel, shapes, specs, *args, flops=0, limit=24, scratch=(), alias=None):
    size = sum(a.size * a.dtype.itemsize for a in args)
    single = not isinstance(shapes, list)
    shapes = [shapes] if single else shapes
    out = pl.pallas_call(
        kernel,
        out_shape=[space(shape, kind) for shape, kind, space in shapes],
        in_specs=specs,
        out_specs=[pl.BlockSpec(memory_space=space) for _, _, space in shapes],
        scratch_shapes=list(scratch),
        input_output_aliases=alias or {},
        cost_estimate=pl.CostEstimate(flops=flops, bytes_accessed=size, transcendentals=0),
        compiler_params=pltpu.CompilerParams(vmem_limit_bytes=limit * MIB),
    )(*args)
    return out[0] if single else out


def half_of(core):
    return pl.ds(pl.multiple_of(core * HALF, HALF), HALF)


def segment(layer, tap_ref):
    return (layer > tap_ref[0]).astype(jnp.int32) + (layer > tap_ref[1]).astype(jnp.int32)


def load_kernel(tap_hbm, delta_hbm, gain_hbm, other_ref, mine_ref, tap_ref, gain_ref, three_ref, sems):
    core = lax.axis_index(CORE)
    pairs = (
        (delta_hbm.at[:, :, half_of(1 - core)], other_ref),
        (delta_hbm.at[:, :, half_of(core)], mine_ref),
        (tap_hbm, tap_ref),
        (gain_hbm, gain_ref),
    )
    copies = [pltpu.make_async_copy(a, b, sems.at[i]) for i, (a, b) in enumerate(pairs)]
    for copy in copies:
        copy.start()
    for copy in copies:
        copy.wait()
    three_ref[0] = (tap_ref[0] // 4 == tap_ref[1] // 4).astype(jnp.int32)


def pair_kernel(tap_ref, mine_ref, other_ref, ends_ref, middle_ref):
    core = lax.axis_index(CORE)
    first = (lax.axis_index(ZQ) * 2 + lax.axis_index(ZP)) * 4
    head, tail = segment(first, tap_ref), segment(first + 3, tap_ref)
    weights = []
    for side in (core, 1 - core):
        for j in range(2):
            at = segment(first + 2 * side + j, tap_ref)
            in_head = at == head
            in_tail = jnp.logical_and(at == tail, tail != head)
            between = jnp.logical_not(jnp.logical_or(in_head, in_tail))
            weights.append([jnp.where(w, 1.0, 0.0).astype(F32) for w in (in_head, in_tail, between)])
    for piece in range(8):
        rows = slice(piece * ROWS, (piece + 1) * ROWS)
        layers = [ref[j, rows].astype(F32) for ref in (mine_ref, other_ref) for j in range(2)]
        sums = []
        for part in range(3):
            terms = [layer * weight[part] for layer, weight in zip(layers, weights)]
            sums.append(((terms[0] + terms[1]) + (terms[2] + terms[3])).astype(BF))
        ends_ref[piece, 0] = sums[0]
        ends_ref[piece, 1] = sums[1]
        middle_ref[piece] = sums[2]


def tapped_kernel(tap_ref, ends_ref, middle_ref, gain_ref, out_ref):
    columns = half_of(lax.axis_index(CORE))
    between = middle_ref[0].astype(F32)
    for chip in range(1, 8):
        between = between + middle_ref[chip].astype(F32)
    for k in range(3):
        state = between if k else jnp.zeros_like(between)
        for chip in range(8):
            for end in range(2):
                inside = jnp.where(4 * chip + 3 * end <= tap_ref[k], 1.0, 0.0).astype(F32)
                state = state + ends_ref[chip, end].astype(F32) * inside
        out_ref[0, k] = (state * gain_ref[pl.ds(k, 1), columns]).astype(BF)


def blocks_of():
    z = 2 * lax.axis_index(ZQ) + lax.axis_index(ZP)
    mine = lax.axis_index(LO) * 8
    yours = 8 - mine
    early = [mine + lax.rem(z + step, 8) for step in (0, 6, 2, 4)] + [yours + z]
    early += [mine + lax.rem(z + 7, 8), mine + lax.rem(z + 5, 8), yours + lax.rem(z + 7, 8)]
    early += [mine + lax.rem(z + 1, 8), mine + lax.rem(z + 3, 8), yours + lax.rem(z + 1, 8)]
    early += [yours + lax.rem(z + step, 8) for step in (2, 6, 4)]
    return early, [yours + lax.rem(z + 5, 8), yours + lax.rem(z + 3, 8)]


def pack_kernel(count, *refs):
    out_ref = refs[-1]
    at = 0
    for ref in refs[:count]:
        out_ref[at : at + ref.shape[0]] = ref[...]
        at += ref.shape[0]


def ends_kernel(across_ref, left_ref, right_ref):
    left_ref[0] = across_ref[0]
    right_ref[0] = across_ref[1]


def fetch_kernel(weight_hbm, after_ref, weight_ref, sem):
    del after_ref
    copy = pltpu.make_async_copy(weight_hbm, weight_ref, sem)
    copy.start()
    copy.wait()


def join(blocks, sides, weight_ref, gain_ref, out_ref, state_ref):
    lane = lax.broadcasted_iota(jnp.int32, (ROWS, 128), 1) // ROWS
    squares = [[None] * 3 for _ in blocks]
    for k in range(3):
        total = None
        sums = None
        for refs, side in sides:
            at = 0
            for ref in refs:
                rows = ref.shape[0] * ROWS
                state_ref[at : at + rows, :] = ref[:, k].reshape(rows, HALF)
                at += rows
            states = state_ref[...]
            product = jnp.dot(states, weight_ref[k, half_of(side), :], preferred_element_type=F32)
            plain = states.astype(F32) * (1.0 / gain_ref[pl.ds(k, 1), half_of(side)])
            square = jnp.sum(plain * plain, axis=1, keepdims=True)
            total = product if total is None else total + product
            sums = square if sums is None else sums + square
        total = total.astype(BF)
        for i, block in enumerate(blocks):
            rows = slice(i * ROWS, (i + 1) * ROWS)
            squares[i][k] = sums[rows]
            for column in range(4):
                at = pl.multiple_of((k * 4 + column) * 32 + lax.rem(block, 2) * ROWS, ROWS)
                out_ref[block // 2, pl.ds(at, ROWS), :] = total[rows, column * 128 : (column + 1) * 128]
    for i, block in enumerate(blocks):
        packed = out_ref[block // 2, 384:400, :].astype(F32)
        for k in range(3):
            packed = jnp.where(lane == 2 * k + lax.rem(block, 2), squares[i][k], packed)
        out_ref[block // 2, 384:400, :] = packed.astype(BF)


def early_kernel(head, middle, head_other, middle_other, weight_ref, gain_ref, out_ref, state_ref):
    core = lax.axis_index(CORE)
    out_ref[:, 384:400, :] = jnp.zeros((8, ROWS, 128), BF)
    sides = (((head, middle), core), ((head_other, middle_other), 1 - core))
    join(blocks_of()[0], sides, weight_ref, gain_ref, out_ref, state_ref)


def last_kernel(early_ref, last, last_other, weight_ref, gain_ref, out_ref, state_ref):
    del early_ref
    core = lax.axis_index(CORE)
    join(blocks_of()[1], (((last,), core), ((last_other,), 1 - core)), weight_ref, gain_ref, out_ref, state_ref)


def scale_kernel(parts_ref, out_ref):
    squares = parts_ref[0, 384:400, :].astype(F32)
    for piece in range(1, 8):
        squares = squares + parts_ref[piece, 384:400, :].astype(F32)
    scale = lax.rsqrt(squares / D + EPS)
    for h in range(2):
        for column in range(4):
            joined = None
            for k in range(3):
                rows = pl.ds((k * 4 + column) * 32 + h * ROWS, ROWS)
                total = parts_ref[0, rows, :].astype(F32)
                for piece in range(1, 8):
                    total = total + parts_ref[piece, rows, :].astype(F32)
                at = ROWS * (2 * k + h)
                total = total * scale[:, at : at + 1]
                joined = total if joined is None else joined + total
            joined = joined.astype(BF)
            for copy in range(8):
                out_ref[copy, h * ROWS : (h + 1) * ROWS, column * 128 : (column + 1) * 128] = joined


def swap(a, axis):
    return lax.ppermute(a, axis, [(0, 1), (1, 0)])


def along(a, step):
    return lax.ppermute(a, Z, [(i, (i + step) % 8) for i in range(8)])


def exchange(a, axes):
    return lax.all_to_all(a, axes, 0, 0, tiled=True)


def states(count):
    return ((count, 3, ROWS, HALF), BF, pltpu.VMEM)


def shards(layer_deltas, tap_layers, norm_gain, fc_weight):
    raw = ((2, 128, HALF), BF, pltpu.VMEM)
    sources = [pltpu.with_memory_space_constraint(a, pltpu.HBM) for a in (tap_layers, layer_deltas, norm_gain)]
    sent, own, taps, gain, three = call(
        load_kernel,
        [
            raw,
            raw,
            (tap_layers.shape, jnp.int32, pltpu.SMEM),
            (norm_gain.shape, F32, pltpu.VMEM),
            ((1,), jnp.int32, pltpu.SMEM),
        ],
        [HBM] * 3,
        *sources,
        scratch=[pltpu.SemaphoreType.DMA((4,))],
    )
    ends, middle = call(
        pair_kernel,
        [((8, 2, ROWS, HALF), BF, pltpu.VMEM), ((8, ROWS, HALF), BF, pltpu.VMEM)],
        [SMEM, VMEM, VMEM],
        taps,
        own,
        swap(sent, CORE),
    )
    ends = exchange(ends, Z)
    middle = lax.cond(three[0] != 0, lambda a: exchange(a, Z), lambda a: a, middle)
    piece = call(tapped_kernel, states(1), [SMEM, VMEM, VMEM, VMEM], taps, ends, middle, gain)
    far = along(piece, 4)
    below, above = along(piece, 2), along(piece, -2)
    near = swap(piece, LO)
    pack = functools.partial(pack_kernel, 3)
    across = call(pack, states(3), [VMEM] * 3, above, below, far)
    right = call(pack, states(3), [VMEM] * 3, piece, below, near)
    left = call(pack, states(3), [VMEM] * 3, piece, above, near)
    pack = functools.partial(pack_kernel, 2)
    head = call(pack, states(2), [VMEM] * 2, piece, below)
    tail = call(pack, states(2), [VMEM] * 2, above, far)
    weight = call(
        fetch_kernel,
        (fc_weight.shape, BF, pltpu.VMEM),
        [HBM, ANY],
        pltpu.with_memory_space_constraint(fc_weight, pltpu.HBM),
        across,
        scratch=[pltpu.SemaphoreType.DMA],
    )
    first = (swap(across, LO), along(right, 1), along(left, -1), swap(head, CORE), weight)
    across, from_left, from_right, head_other, weight = lax.optimization_barrier(first)
    left, right = call(ends_kernel, [states(1)] * 2, [VMEM], across)
    far_left, far_right = along(right, 1), along(left, -1)
    pack = functools.partial(pack_kernel, 5)
    middle = call(pack, states(12), [VMEM] * 5, tail, near, from_left, from_right, across)
    payload = ((8, 400, 128), BF, pltpu.VMEM)
    partial = call(
        early_kernel,
        payload,
        [VMEM] * 6,
        head,
        middle,
        head_other,
        swap(middle, CORE),
        weight,
        gain,
        flops=2 * 224 * 6144 * 512,
        scratch=[pltpu.VMEM((224, HALF), BF)],
    )
    pack = functools.partial(pack_kernel, 2)
    last = call(pack, states(2), [VMEM, VMEM, ANY], far_left, far_right, partial)
    partial = call(
        last_kernel,
        payload,
        [VMEM] * 5,
        partial,
        last,
        swap(last, CORE),
        weight,
        gain,
        flops=2 * 32 * 6144 * 512,
        scratch=[pltpu.VMEM((32, HALF), BF)],
        alias={0: 0},
    )
    partial = exchange(partial, (X, HI))
    joined = call(scale_kernel, ((8, 32, 512), BF, pltpu.VMEM), [VMEM], partial)
    return exchange(joined, (X, HI)).reshape(256, 512)


def solution(mesh):
    fine = Mesh(mesh.devices.reshape(4, 2, 2, 2, 4, 2), (ZQ, ZP, CORE, HI, X, LO))
    section, tensor = (ZQ, ZP, CORE), (HI, X)
    in_specs = (P(section, LO, tensor), P(), P(None, tensor), P(None, tensor, (*section, LO)))
    out_specs = P(None, (*section, LO))
    return jax.shard_map(shards, mesh=fine, in_specs=in_specs, out_specs=out_specs, check_vma=False)
```

```python
import functools

import jax
import jax.numpy as jnp
from jax import lax
from jax.experimental import pallas as pl
from jax.experimental.pallas import tpu as pltpu
from jax.sharding import Mesh, PartitionSpec as P

D = 16384
EPS = 1e-05
ZQ, ZP, CORE, HI, X, LO = "zq", "zp", "core", "hi", "x", "lo"
Z = (ZQ, ZP)
BF, F32 = jnp.bfloat16, jnp.float32
ROWS = 16
HALF = 1024
MIB = 1 << 20

VMEM = pl.BlockSpec(memory_space=pltpu.VMEM)
SMEM = pl.BlockSpec(memory_space=pltpu.SMEM)
HBM = pl.BlockSpec(memory_space=pltpu.HBM)
ANY = pl.BlockSpec(memory_space=pl.ANY)


def call(kernel, shapes, specs, *args, flops=0, limit=24, scratch=(), alias=None):
    size = sum(a.size * a.dtype.itemsize for a in args)
    single = not isinstance(shapes, list)
    shapes = [shapes] if single else shapes
    out = pl.pallas_call(
        kernel,
        out_shape=[space(shape, kind) for shape, kind, space in shapes],
        in_specs=specs,
        out_specs=[pl.BlockSpec(memory_space=space) for _, _, space in shapes],
        scratch_shapes=list(scratch),
        input_output_aliases=alias or {},
        cost_estimate=pl.CostEstimate(flops=flops, bytes_accessed=size, transcendentals=0),
        compiler_params=pltpu.CompilerParams(vmem_limit_bytes=limit * MIB),
    )(*args)
    return out[0] if single else out


def half_of(core):
    return pl.ds(pl.multiple_of(core * HALF, HALF), HALF)


def segment(layer, tap_ref):
    return (layer > tap_ref[0]).astype(jnp.int32) + (layer > tap_ref[1]).astype(jnp.int32)


def load_kernel(tap_hbm, delta_hbm, gain_hbm, other_ref, mine_ref, tap_ref, gain_ref, three_ref, sems):
    core = lax.axis_index(CORE)
    pairs = (
        (delta_hbm.at[:, :, half_of(1 - core)], other_ref),
        (delta_hbm.at[:, :, half_of(core)], mine_ref),
        (tap_hbm, tap_ref),
        (gain_hbm, gain_ref),
    )
    copies = [pltpu.make_async_copy(a, b, sems.at[i]) for i, (a, b) in enumerate(pairs)]
    for copy in copies:
        copy.start()
    for copy in copies:
        copy.wait()
    three_ref[0] = (tap_ref[0] // 4 == tap_ref[1] // 4).astype(jnp.int32)


def pair_kernel(tap_ref, mine_ref, other_ref, ends_ref, middle_ref):
    core = lax.axis_index(CORE)
    first = (lax.axis_index(ZQ) * 2 + lax.axis_index(ZP)) * 4
    head, tail = segment(first, tap_ref), segment(first + 3, tap_ref)
    weights = []
    for side in (core, 1 - core):
        for j in range(2):
            at = segment(first + 2 * side + j, tap_ref)
            in_head = at == head
            in_tail = jnp.logical_and(at == tail, tail != head)
            between = jnp.logical_not(jnp.logical_or(in_head, in_tail))
            weights.append([jnp.where(w, 1.0, 0.0).astype(F32) for w in (in_head, in_tail, between)])
    for piece in range(8):
        rows = slice(piece * ROWS, (piece + 1) * ROWS)
        layers = [ref[j, rows].astype(F32) for ref in (mine_ref, other_ref) for j in range(2)]
        sums = []
        for part in range(3):
            terms = [layer * weight[part] for layer, weight in zip(layers, weights)]
            sums.append(((terms[0] + terms[1]) + (terms[2] + terms[3])).astype(BF))
        ends_ref[piece, 0] = sums[0]
        ends_ref[piece, 1] = sums[1]
        middle_ref[piece] = sums[2]


def tapped_kernel(tap_ref, ends_ref, middle_ref, gain_ref, out_ref):
    columns = half_of(lax.axis_index(CORE))
    between = middle_ref[0].astype(F32)
    for chip in range(1, 8):
        between = between + middle_ref[chip].astype(F32)
    for k in range(3):
        state = between if k else jnp.zeros_like(between)
        for chip in range(8):
            for end in range(2):
                inside = jnp.where(4 * chip + 3 * end <= tap_ref[k], 1.0, 0.0).astype(F32)
                state = state + ends_ref[chip, end].astype(F32) * inside
        out_ref[0, k] = (state * gain_ref[pl.ds(k, 1), columns]).astype(BF)


def blocks_of():
    z = 2 * lax.axis_index(ZQ) + lax.axis_index(ZP)
    mine = lax.axis_index(LO) * 8
    yours = 8 - mine
    early = [mine + lax.rem(z + step, 8) for step in (0, 6, 2, 4)] + [yours + z]
    early += [mine + lax.rem(z + 7, 8), mine + lax.rem(z + 5, 8), yours + lax.rem(z + 7, 8)]
    early += [mine + lax.rem(z + 1, 8), mine + lax.rem(z + 3, 8), yours + lax.rem(z + 1, 8)]
    early += [yours + lax.rem(z + step, 8) for step in (2, 6, 4)]
    return early, [yours + lax.rem(z + 5, 8), yours + lax.rem(z + 3, 8)]


def pack_kernel(count, *refs):
    out_ref = refs[-1]
    at = 0
    for ref in refs[:count]:
        out_ref[at : at + ref.shape[0]] = ref[...]
        at += ref.shape[0]


def ends_kernel(across_ref, left_ref, right_ref):
    left_ref[0] = across_ref[0]
    right_ref[0] = across_ref[1]


def fetch_kernel(weight_hbm, after_ref, weight_ref, sem):
    del after_ref
    copy = pltpu.make_async_copy(weight_hbm, weight_ref, sem)
    copy.start()
    copy.wait()


def join(blocks, sides, weight_ref, gain_ref, out_ref, state_ref, product_ref=None, square_ref=None):
    lane = lax.broadcasted_iota(jnp.int32, (ROWS, 128), 1) // ROWS
    squares = [[None] * 3 for _ in blocks]
    for k in range(3):
        total = None if product_ref is None else product_ref[k]
        sums = None if square_ref is None else square_ref[:, k : k + 1]
        for refs, side in sides:
            at = 0
            for ref in refs:
                rows = ref.shape[0] * ROWS
                state_ref[at : at + rows, :] = ref[:, k].reshape(rows, HALF)
                at += rows
            states = state_ref[...]
            product = jnp.dot(states, weight_ref[k, half_of(side), :], preferred_element_type=F32)
            plain = states.astype(F32) * (1.0 / gain_ref[pl.ds(k, 1), half_of(side)])
            square = jnp.sum(plain * plain, axis=1, keepdims=True)
            total = product if total is None else total + product
            sums = square if sums is None else sums + square
        total = total.astype(BF)
        for i, block in enumerate(blocks):
            rows = slice(i * ROWS, (i + 1) * ROWS)
            squares[i][k] = sums[rows]
            for column in range(4):
                at = pl.multiple_of((k * 4 + column) * 32 + lax.rem(block, 2) * ROWS, ROWS)
                out_ref[block // 2, pl.ds(at, ROWS), :] = total[rows, column * 128 : (column + 1) * 128]
    for i, block in enumerate(blocks):
        packed = out_ref[block // 2, 384:400, :].astype(F32)
        for k in range(3):
            packed = jnp.where(lane == 2 * k + lax.rem(block, 2), squares[i][k], packed)
        out_ref[block // 2, 384:400, :] = packed.astype(BF)


def early_kernel(head, middle, head_other, middle_other, weight_ref, gain_ref, out_ref, state_ref):
    core = lax.axis_index(CORE)
    out_ref[:, 384:400, :] = jnp.zeros((8, ROWS, 128), BF)
    sides = (((head, middle), core), ((head_other, middle_other), 1 - core))
    join(blocks_of()[0], sides, weight_ref, gain_ref, out_ref, state_ref)


def last_mine_kernel(last, weight_ref, gain_ref, product_ref, square_ref, state_ref):
    lane = lax.broadcasted_iota(jnp.int32, square_ref.shape, 1)
    side = half_of(lax.axis_index(CORE))
    squares = jnp.zeros(square_ref.shape, F32)
    for k in range(3):
        state_ref[...] = last[:, k].reshape(state_ref.shape)
        states = state_ref[...]
        product_ref[k] = jnp.dot(states, weight_ref[k, side, :], preferred_element_type=F32)
        plain = states.astype(F32) * (1.0 / gain_ref[pl.ds(k, 1), side])
        squares = jnp.where(lane == k, jnp.sum(plain * plain, axis=1, keepdims=True), squares)
    square_ref[...] = squares


def last_kernel(early_ref, last_other, product_ref, square_ref, weight_ref, gain_ref, out_ref, state_ref):
    del early_ref
    sides = (((last_other,), 1 - lax.axis_index(CORE)),)
    join(blocks_of()[1], sides, weight_ref, gain_ref, out_ref, state_ref, product_ref, square_ref)


def scale_kernel(parts_ref, out_ref):
    squares = parts_ref[0, 384:400, :].astype(F32)
    for piece in range(1, 8):
        squares = squares + parts_ref[piece, 384:400, :].astype(F32)
    scale = lax.rsqrt(squares / D + EPS)
    for h in range(2):
        for column in range(4):
            joined = None
            for k in range(3):
                rows = pl.ds((k * 4 + column) * 32 + h * ROWS, ROWS)
                total = parts_ref[0, rows, :].astype(F32)
                for piece in range(1, 8):
                    total = total + parts_ref[piece, rows, :].astype(F32)
                at = ROWS * (2 * k + h)
                total = total * scale[:, at : at + 1]
                joined = total if joined is None else joined + total
            joined = joined.astype(BF)
            for copy in range(8):
                out_ref[copy, h * ROWS : (h + 1) * ROWS, column * 128 : (column + 1) * 128] = joined


def swap(a, axis):
    return lax.ppermute(a, axis, [(0, 1), (1, 0)])


def along(a, step):
    return lax.ppermute(a, Z, [(i, (i + step) % 8) for i in range(8)])


def exchange(a, axes):
    return lax.all_to_all(a, axes, 0, 0, tiled=True)


def reduce_two(ends, middle):
    return exchange(ends, Z), middle


def reduce_three(ends, middle):
    parts = exchange(jnp.concatenate([ends, middle[:, None]], axis=1), Z)
    return parts[:, :2], parts[:, 2]


def states(count):
    return ((count, 3, ROWS, HALF), BF, pltpu.VMEM)


def shards(layer_deltas, tap_layers, norm_gain, fc_weight):
    raw = ((2, 128, HALF), BF, pltpu.VMEM)
    sources = [pltpu.with_memory_space_constraint(a, pltpu.HBM) for a in (tap_layers, layer_deltas, norm_gain)]
    sent, own, taps, gain, three = call(
        load_kernel,
        [
            raw,
            raw,
            (tap_layers.shape, jnp.int32, pltpu.SMEM),
            (norm_gain.shape, F32, pltpu.VMEM),
            ((1,), jnp.int32, pltpu.SMEM),
        ],
        [HBM] * 3,
        *sources,
        scratch=[pltpu.SemaphoreType.DMA((4,))],
    )
    ends, middle = call(
        pair_kernel,
        [((8, 2, ROWS, HALF), BF, pltpu.VMEM), ((8, ROWS, HALF), BF, pltpu.VMEM)],
        [SMEM, VMEM, VMEM],
        taps,
        own,
        swap(sent, CORE),
    )
    ends, middle = lax.cond(three[0] != 0, reduce_three, reduce_two, ends, middle)
    piece = call(tapped_kernel, states(1), [SMEM, VMEM, VMEM, VMEM], taps, ends, middle, gain)
    far = along(piece, 4)
    below, above = along(piece, 2), along(piece, -2)
    near = swap(piece, LO)
    pack = functools.partial(pack_kernel, 3)
    across = call(pack, states(3), [VMEM] * 3, above, below, far)
    right = call(pack, states(3), [VMEM] * 3, piece, below, near)
    left = call(pack, states(3), [VMEM] * 3, piece, above, near)
    pack = functools.partial(pack_kernel, 2)
    head = call(pack, states(2), [VMEM] * 2, piece, below)
    tail = call(pack, states(2), [VMEM] * 2, above, far)
    weight = call(
        fetch_kernel,
        (fc_weight.shape, BF, pltpu.VMEM),
        [HBM, ANY],
        pltpu.with_memory_space_constraint(fc_weight, pltpu.HBM),
        across,
        scratch=[pltpu.SemaphoreType.DMA],
    )
    first = (swap(across, LO), along(right, 1), along(left, -1), swap(head, CORE), weight)
    across, from_left, from_right, head_other, weight = lax.optimization_barrier(first)
    left, right = call(ends_kernel, [states(1)] * 2, [VMEM], across)
    far_left, far_right = along(right, 1), along(left, -1)
    pack = functools.partial(pack_kernel, 5)
    middle = call(pack, states(12), [VMEM] * 5, tail, near, from_left, from_right, across)
    payload = ((8, 400, 128), BF, pltpu.VMEM)
    partial = call(
        early_kernel,
        payload,
        [VMEM] * 6,
        head,
        middle,
        head_other,
        swap(middle, CORE),
        weight,
        gain,
        flops=2 * 224 * 6144 * 512,
        scratch=[pltpu.VMEM((224, HALF), BF)],
    )
    pack = functools.partial(pack_kernel, 2)
    last = call(pack, states(2), [VMEM, VMEM, ANY], far_left, far_right, partial)
    product, square = call(
        last_mine_kernel,
        [((3, 32, 512), F32, pltpu.VMEM), ((32, 128), F32, pltpu.VMEM)],
        [VMEM] * 3,
        last,
        weight,
        gain,
        flops=32 * 6144 * 512,
        scratch=[pltpu.VMEM((32, HALF), BF)],
    )
    partial = call(
        last_kernel,
        payload,
        [VMEM] * 6,
        partial,
        swap(last, CORE),
        product,
        square,
        weight,
        gain,
        flops=32 * 6144 * 512,
        scratch=[pltpu.VMEM((32, HALF), BF)],
        alias={0: 0},
    )
    partial = exchange(partial, (X, HI))
    joined = call(scale_kernel, ((8, 32, 512), BF, pltpu.VMEM), [VMEM], partial)
    return exchange(joined, (X, HI)).reshape(256, 512)


def solution(mesh):
    fine = Mesh(mesh.devices.reshape(4, 2, 2, 2, 4, 2), (ZQ, ZP, CORE, HI, X, LO))
    section, tensor = (ZQ, ZP, CORE), (HI, X)
    in_specs = (P(section, LO, tensor), P(), P(None, tensor), P(None, tensor, (*section, LO)))
    out_specs = P(None, (*section, LO))
    return jax.shard_map(shards, mesh=fine, in_specs=in_specs, out_specs=out_specs, check_vma=False)
```

```python
import functools

import jax
import jax.numpy as jnp
from jax import lax
from jax.experimental import pallas as pl
from jax.experimental.pallas import tpu as pltpu
from jax.sharding import Mesh, PartitionSpec as P

D = 16384
EPS = 1e-05
ZQ, ZP, CORE, HI, X, LO = "zq", "zp", "core", "hi", "x", "lo"
Z = (ZQ, ZP)
BF, F32 = jnp.bfloat16, jnp.float32
ROWS = 16
HALF = 1024
MIB = 1 << 20

VMEM = pl.BlockSpec(memory_space=pltpu.VMEM)
SMEM = pl.BlockSpec(memory_space=pltpu.SMEM)
HBM = pl.BlockSpec(memory_space=pltpu.HBM)
ANY = pl.BlockSpec(memory_space=pl.ANY)


def call(kernel, shapes, specs, *args, flops=0, limit=24, scratch=(), alias=None):
    size = sum(a.size * a.dtype.itemsize for a in args)
    single = not isinstance(shapes, list)
    shapes = [shapes] if single else shapes
    out = pl.pallas_call(
        kernel,
        out_shape=[space(shape, kind) for shape, kind, space in shapes],
        in_specs=specs,
        out_specs=[pl.BlockSpec(memory_space=space) for _, _, space in shapes],
        scratch_shapes=list(scratch),
        input_output_aliases=alias or {},
        cost_estimate=pl.CostEstimate(flops=flops, bytes_accessed=size, transcendentals=0),
        compiler_params=pltpu.CompilerParams(vmem_limit_bytes=limit * MIB),
    )(*args)
    return out[0] if single else out


def half_of(core):
    return pl.ds(pl.multiple_of(core * HALF, HALF), HALF)


def segment(layer, tap_ref):
    return (layer > tap_ref[0]).astype(jnp.int32) + (layer > tap_ref[1]).astype(jnp.int32)


def load_kernel(tap_hbm, delta_hbm, gain_hbm, other_ref, mine_ref, tap_ref, gain_ref, three_ref, sems):
    core = lax.axis_index(CORE)
    pairs = (
        (delta_hbm.at[:, :, half_of(1 - core)], other_ref),
        (delta_hbm.at[:, :, half_of(core)], mine_ref),
        (tap_hbm, tap_ref),
        (gain_hbm, gain_ref),
    )
    copies = [pltpu.make_async_copy(a, b, sems.at[i]) for i, (a, b) in enumerate(pairs)]
    for copy in copies:
        copy.start()
    for copy in copies:
        copy.wait()
    three_ref[0] = (tap_ref[0] // 4 == tap_ref[1] // 4).astype(jnp.int32)


def pair_kernel(tap_ref, mine_ref, other_ref, ends_ref, middle_ref):
    core = lax.axis_index(CORE)
    first = (lax.axis_index(ZQ) * 2 + lax.axis_index(ZP)) * 4
    head, tail = segment(first, tap_ref), segment(first + 3, tap_ref)
    weights = []
    for side in (core, 1 - core):
        for j in range(2):
            at = segment(first + 2 * side + j, tap_ref)
            in_head = at == head
            in_tail = jnp.logical_and(at == tail, tail != head)
            between = jnp.logical_not(jnp.logical_or(in_head, in_tail))
            weights.append([jnp.where(w, 1.0, 0.0).astype(F32) for w in (in_head, in_tail, between)])
    for piece in range(8):
        rows = slice(piece * ROWS, (piece + 1) * ROWS)
        layers = [ref[j, rows].astype(F32) for ref in (mine_ref, other_ref) for j in range(2)]
        sums = []
        for part in range(3):
            terms = [layer * weight[part] for layer, weight in zip(layers, weights)]
            sums.append(((terms[0] + terms[1]) + (terms[2] + terms[3])).astype(BF))
        ends_ref[piece, 0] = sums[0]
        ends_ref[piece, 1] = sums[1]
        middle_ref[piece] = sums[2]


def tapped_kernel(tap_ref, ends_ref, middle_ref, gain_ref, out_ref):
    columns = half_of(lax.axis_index(CORE))
    between = middle_ref[0].astype(F32)
    for chip in range(1, 8):
        between = between + middle_ref[chip].astype(F32)
    for k in range(3):
        state = between if k else jnp.zeros_like(between)
        for slot in range(8):
            chip = 2 * (slot % 4) + slot // 4
            for end in range(2):
                inside = jnp.where(4 * chip + 3 * end <= tap_ref[k], 1.0, 0.0).astype(F32)
                state = state + ends_ref[slot, end].astype(F32) * inside
        out_ref[0, k] = (state * gain_ref[pl.ds(k, 1), columns]).astype(BF)


def blocks_of():
    z = 2 * lax.axis_index(ZQ) + lax.axis_index(ZP)
    mine = lax.axis_index(LO) * 8

    def block(group, step):
        chip = lax.rem(z + step, 8)
        return group + lax.rem(chip, 2) * 4 + chip // 2

    yours = 8 - mine
    early = [block(mine, step) for step in (0, 6, 2, 4)] + [block(yours, 0)]
    early += [block(mine, 7), block(mine, 5), block(yours, 7)]
    early += [block(mine, 1), block(mine, 3), block(yours, 1)]
    early += [block(yours, step) for step in (2, 6, 4)]
    return early, [block(yours, 5), block(yours, 3)]


def pack_kernel(count, *refs):
    out_ref = refs[-1]
    at = 0
    for ref in refs[:count]:
        out_ref[at : at + ref.shape[0]] = ref[...]
        at += ref.shape[0]


def ends_kernel(across_ref, left_ref, right_ref):
    left_ref[0] = across_ref[0]
    right_ref[0] = across_ref[1]


def fetch_kernel(weight_hbm, after_ref, weight_ref, sem):
    del after_ref
    copy = pltpu.make_async_copy(weight_hbm, weight_ref, sem)
    copy.start()
    copy.wait()


def join(blocks, sides, weight_ref, gain_ref, out_ref, state_ref, product_ref=None, square_ref=None):
    lane = lax.broadcasted_iota(jnp.int32, (ROWS, 128), 1) // ROWS
    squares = [[None] * 3 for _ in blocks]
    for k in range(3):
        total = None if product_ref is None else product_ref[k]
        sums = None if square_ref is None else square_ref[:, k : k + 1]
        for refs, side in sides:
            at = 0
            for ref in refs:
                rows = ref.shape[0] * ROWS
                state_ref[at : at + rows, :] = ref[:, k].reshape(rows, HALF)
                at += rows
            states = state_ref[...]
            product = jnp.dot(states, weight_ref[k, half_of(side), :], preferred_element_type=F32)
            plain = states.astype(F32) * (1.0 / gain_ref[pl.ds(k, 1), half_of(side)])
            square = jnp.sum(plain * plain, axis=1, keepdims=True)
            total = product if total is None else total + product
            sums = square if sums is None else sums + square
        total = total.astype(BF)
        for i, block in enumerate(blocks):
            rows = slice(i * ROWS, (i + 1) * ROWS)
            squares[i][k] = sums[rows]
            for column in range(4):
                at = pl.multiple_of((k * 4 + column) * 32 + lax.rem(block, 2) * ROWS, ROWS)
                out_ref[block // 2, pl.ds(at, ROWS), :] = total[rows, column * 128 : (column + 1) * 128]
    for i, block in enumerate(blocks):
        packed = out_ref[block // 2, 384:400, :].astype(F32)
        for k in range(3):
            packed = jnp.where(lane == 2 * k + lax.rem(block, 2), squares[i][k], packed)
        out_ref[block // 2, 384:400, :] = packed.astype(BF)


def early_kernel(head, middle, head_other, middle_other, weight_ref, gain_ref, out_ref, state_ref):
    core = lax.axis_index(CORE)
    out_ref[:, 384:400, :] = jnp.zeros((8, ROWS, 128), BF)
    sides = (((head, middle), core), ((head_other, middle_other), 1 - core))
    join(blocks_of()[0], sides, weight_ref, gain_ref, out_ref, state_ref)


def last_mine_kernel(last, weight_ref, gain_ref, product_ref, square_ref, state_ref):
    lane = lax.broadcasted_iota(jnp.int32, square_ref.shape, 1)
    side = half_of(lax.axis_index(CORE))
    squares = jnp.zeros(square_ref.shape, F32)
    for k in range(3):
        state_ref[...] = last[:, k].reshape(state_ref.shape)
        states = state_ref[...]
        product_ref[k] = jnp.dot(states, weight_ref[k, side, :], preferred_element_type=F32)
        plain = states.astype(F32) * (1.0 / gain_ref[pl.ds(k, 1), side])
        squares = jnp.where(lane == k, jnp.sum(plain * plain, axis=1, keepdims=True), squares)
    square_ref[...] = squares


def last_kernel(early_ref, last_other, product_ref, square_ref, weight_ref, gain_ref, out_ref, state_ref):
    del early_ref
    sides = (((last_other,), 1 - lax.axis_index(CORE)),)
    join(blocks_of()[1], sides, weight_ref, gain_ref, out_ref, state_ref, product_ref, square_ref)


def scale_kernel(parts_ref, out_ref):
    squares = parts_ref[0, 384:400, :].astype(F32)
    for piece in range(1, 8):
        squares = squares + parts_ref[piece, 384:400, :].astype(F32)
    scale = lax.rsqrt(squares / D + EPS)
    for h in range(2):
        for column in range(4):
            joined = None
            for k in range(3):
                rows = pl.ds((k * 4 + column) * 32 + h * ROWS, ROWS)
                total = parts_ref[0, rows, :].astype(F32)
                for piece in range(1, 8):
                    total = total + parts_ref[piece, rows, :].astype(F32)
                at = ROWS * (2 * k + h)
                total = total * scale[:, at : at + 1]
                joined = total if joined is None else joined + total
            joined = joined.astype(BF)
            for copy in range(8):
                out_ref[copy, h * ROWS : (h + 1) * ROWS, column * 128 : (column + 1) * 128] = joined


def swap(a, axis):
    return lax.ppermute(a, axis, [(0, 1), (1, 0)])


def along(a, step):
    return lax.ppermute(a, Z, [(i, (i + step) % 8) for i in range(8)])


def exchange(a, axes):
    return lax.all_to_all(a, axes, 0, 0, tiled=True)


def reduce_two(ends, middle):
    return exchange(ends, (ZP, ZQ)), middle


def reduce_three(ends, middle):
    parts = exchange(jnp.concatenate([ends, middle[:, None]], axis=1), (ZP, ZQ))
    return parts[:, :2], parts[:, 2]


def states(count):
    return ((count, 3, ROWS, HALF), BF, pltpu.VMEM)


def shards(layer_deltas, tap_layers, norm_gain, fc_weight):
    raw = ((2, 128, HALF), BF, pltpu.VMEM)
    sources = [pltpu.with_memory_space_constraint(a, pltpu.HBM) for a in (tap_layers, layer_deltas, norm_gain)]
    sent, own, taps, gain, three = call(
        load_kernel,
        [
            raw,
            raw,
            (tap_layers.shape, jnp.int32, pltpu.SMEM),
            (norm_gain.shape, F32, pltpu.VMEM),
            ((1,), jnp.int32, pltpu.SMEM),
        ],
        [HBM] * 3,
        *sources,
        scratch=[pltpu.SemaphoreType.DMA((4,))],
    )
    ends, middle = call(
        pair_kernel,
        [((8, 2, ROWS, HALF), BF, pltpu.VMEM), ((8, ROWS, HALF), BF, pltpu.VMEM)],
        [SMEM, VMEM, VMEM],
        taps,
        own,
        swap(sent, CORE),
    )
    ends, middle = lax.cond(three[0] != 0, reduce_three, reduce_two, ends, middle)
    piece = call(tapped_kernel, states(1), [SMEM, VMEM, VMEM, VMEM], taps, ends, middle, gain)
    far = along(piece, 4)
    below, above = along(piece, 2), along(piece, -2)
    near = swap(piece, LO)
    pack = functools.partial(pack_kernel, 3)
    across = call(pack, states(3), [VMEM] * 3, above, below, far)
    right = call(pack, states(3), [VMEM] * 3, piece, below, near)
    left = call(pack, states(3), [VMEM] * 3, piece, above, near)
    pack = functools.partial(pack_kernel, 2)
    head = call(pack, states(2), [VMEM] * 2, piece, below)
    tail = call(pack, states(2), [VMEM] * 2, above, far)
    weight = call(
        fetch_kernel,
        (fc_weight.shape, BF, pltpu.VMEM),
        [HBM, ANY],
        pltpu.with_memory_space_constraint(fc_weight, pltpu.HBM),
        across,
        scratch=[pltpu.SemaphoreType.DMA],
    )
    first = (swap(across, LO), along(right, 1), along(left, -1), swap(head, CORE), weight)
    across, from_left, from_right, head_other, weight = lax.optimization_barrier(first)
    left, right = call(ends_kernel, [states(1)] * 2, [VMEM], across)
    far_left, far_right = along(right, 1), along(left, -1)
    pack = functools.partial(pack_kernel, 5)
    middle = call(pack, states(12), [VMEM] * 5, tail, near, from_left, from_right, across)
    payload = ((8, 400, 128), BF, pltpu.VMEM)
    partial = call(
        early_kernel,
        payload,
        [VMEM] * 6,
        head,
        middle,
        head_other,
        swap(middle, CORE),
        weight,
        gain,
        flops=2 * 224 * 6144 * 512,
        scratch=[pltpu.VMEM((224, HALF), BF)],
    )
    pack = functools.partial(pack_kernel, 2)
    last = call(pack, states(2), [VMEM, VMEM, ANY], far_left, far_right, partial)
    product, square = call(
        last_mine_kernel,
        [((3, 32, 512), F32, pltpu.VMEM), ((32, 128), F32, pltpu.VMEM)],
        [VMEM] * 3,
        last,
        weight,
        gain,
        flops=32 * 6144 * 512,
        scratch=[pltpu.VMEM((32, HALF), BF)],
    )
    partial = call(
        last_kernel,
        payload,
        [VMEM] * 6,
        partial,
        swap(last, CORE),
        product,
        square,
        weight,
        gain,
        flops=32 * 6144 * 512,
        scratch=[pltpu.VMEM((32, HALF), BF)],
        alias={0: 0},
    )
    partial = exchange(partial, (X, HI))
    joined = call(scale_kernel, ((8, 32, 512), BF, pltpu.VMEM), [VMEM], partial)
    return exchange(joined, (X, HI)).reshape(256, 512)


def solution(mesh):
    fine = Mesh(mesh.devices.reshape(4, 2, 2, 2, 4, 2), (ZQ, ZP, CORE, HI, X, LO))
    section, tensor = (ZQ, ZP, CORE), (HI, X)
    in_specs = (P(section, LO, tensor), P(), P(None, tensor), P(None, tensor, (*section, LO)))
    out_specs = P(None, (*section, LO))
    return jax.shard_map(shards, mesh=fine, in_specs=in_specs, out_specs=out_specs, check_vma=False)
```

```python
import functools

import jax
import jax.numpy as jnp
from jax import lax
from jax.experimental import pallas as pl
from jax.experimental.pallas import tpu as pltpu
from jax.sharding import Mesh, PartitionSpec as P

D = 16384
EPS = 1e-05
ZQ, ZP, CORE, HI, X, LO = "zq", "zp", "core", "hi", "x", "lo"
Z = (ZQ, ZP)
BF, F32 = jnp.bfloat16, jnp.float32
ROWS = 16
HALF = 1024
MIB = 1 << 20

VMEM = pl.BlockSpec(memory_space=pltpu.VMEM)
SMEM = pl.BlockSpec(memory_space=pltpu.SMEM)
HBM = pl.BlockSpec(memory_space=pltpu.HBM)
ANY = pl.BlockSpec(memory_space=pl.ANY)


def call(kernel, shapes, specs, *args, flops=0, limit=24, scratch=(), alias=None):
    size = sum(a.size * a.dtype.itemsize for a in args)
    single = not isinstance(shapes, list)
    shapes = [shapes] if single else shapes
    out = pl.pallas_call(
        kernel,
        out_shape=[space(shape, kind) for shape, kind, space in shapes],
        in_specs=specs,
        out_specs=[pl.BlockSpec(memory_space=space) for _, _, space in shapes],
        scratch_shapes=list(scratch),
        input_output_aliases=alias or {},
        cost_estimate=pl.CostEstimate(flops=flops, bytes_accessed=size, transcendentals=0),
        compiler_params=pltpu.CompilerParams(vmem_limit_bytes=limit * MIB),
    )(*args)
    return out[0] if single else out


def half_of(core):
    return pl.ds(pl.multiple_of(core * HALF, HALF), HALF)


def segment(layer, tap_ref):
    return (layer > tap_ref[0]).astype(jnp.int32) + (layer > tap_ref[1]).astype(jnp.int32)


def load_other_kernel(delta_hbm, other_ref, sem):
    copy = pltpu.make_async_copy(delta_hbm.at[:, :, half_of(1 - lax.axis_index(CORE))], other_ref, sem)
    copy.start()
    copy.wait()


def load_kernel(tap_hbm, delta_hbm, gain_hbm, after_ref, mine_ref, tap_ref, gain_ref, three_ref, sems):
    del after_ref
    core = lax.axis_index(CORE)
    pairs = (
        (delta_hbm.at[:, :, half_of(core)], mine_ref),
        (tap_hbm, tap_ref),
        (gain_hbm, gain_ref),
    )
    copies = [pltpu.make_async_copy(a, b, sems.at[i]) for i, (a, b) in enumerate(pairs)]
    for copy in copies:
        copy.start()
    for copy in copies:
        copy.wait()
    three_ref[0] = (tap_ref[0] // 4 == tap_ref[1] // 4).astype(jnp.int32)


def pair_kernel(tap_ref, mine_ref, other_ref, ends_ref, middle_ref):
    core = lax.axis_index(CORE)
    first = (lax.axis_index(ZQ) * 2 + lax.axis_index(ZP)) * 4
    head, tail = segment(first, tap_ref), segment(first + 3, tap_ref)
    weights = []
    for side in (core, 1 - core):
        for j in range(2):
            at = segment(first + 2 * side + j, tap_ref)
            in_head = at == head
            in_tail = jnp.logical_and(at == tail, tail != head)
            between = jnp.logical_not(jnp.logical_or(in_head, in_tail))
            weights.append([jnp.where(w, 1.0, 0.0).astype(F32) for w in (in_head, in_tail, between)])
    for piece in range(8):
        rows = slice(piece * ROWS, (piece + 1) * ROWS)
        layers = [ref[j, rows].astype(F32) for ref in (mine_ref, other_ref) for j in range(2)]
        sums = []
        for part in range(3):
            terms = [layer * weight[part] for layer, weight in zip(layers, weights)]
            sums.append(((terms[0] + terms[1]) + (terms[2] + terms[3])).astype(BF))
        ends_ref[piece, 0] = sums[0]
        ends_ref[piece, 1] = sums[1]
        middle_ref[piece] = sums[2]


def tapped_kernel(tap_ref, ends_ref, middle_ref, gain_ref, out_ref):
    columns = half_of(lax.axis_index(CORE))
    between = middle_ref[0].astype(F32)
    for chip in range(1, 8):
        between = between + middle_ref[chip].astype(F32)
    for k in range(3):
        state = between if k else jnp.zeros_like(between)
        for slot in range(8):
            chip = 2 * (slot % 4) + slot // 4
            for end in range(2):
                inside = jnp.where(4 * chip + 3 * end <= tap_ref[k], 1.0, 0.0).astype(F32)
                state = state + ends_ref[slot, end].astype(F32) * inside
        out_ref[0, k] = (state * gain_ref[pl.ds(k, 1), columns]).astype(BF)


def blocks_of():
    z = 2 * lax.axis_index(ZQ) + lax.axis_index(ZP)
    mine = lax.axis_index(LO) * 8

    def block(group, step):
        chip = lax.rem(z + step, 8)
        return group + lax.rem(chip, 2) * 4 + chip // 2

    yours = 8 - mine
    early = [block(mine, step) for step in (0, 6, 2)] + [block(yours, 0)]
    early += [block(mine, 7), block(mine, 5), block(yours, 7)]
    early += [block(mine, 1), block(mine, 3), block(yours, 1)]
    early += [block(yours, 2), block(yours, 6), block(mine, 4)]
    return early, [block(yours, 4), block(yours, 5), block(yours, 3)]


def halves_kernel(above, below, up_ref, down_ref):
    up_ref[...] = above[:, :, :, : HALF // 2]
    down_ref[...] = below[:, :, :, HALF // 2 :]


def far_kernel(up, down, far_ref):
    far_ref[:, :, :, : HALF // 2] = up[...]
    far_ref[:, :, :, HALF // 2 :] = down[...]


def pack_kernel(count, *refs):
    out_ref = refs[-1]
    at = 0
    for ref in refs[:count]:
        out_ref[at : at + ref.shape[0]] = ref[...]
        at += ref.shape[0]


def ends_kernel(across_ref, left_ref, right_ref):
    left_ref[0] = across_ref[0]
    right_ref[0] = across_ref[1]


def fetch_kernel(weight_hbm, after_ref, weight_ref, sem):
    del after_ref
    copy = pltpu.make_async_copy(weight_hbm, weight_ref, sem)
    copy.start()
    copy.wait()


def join(blocks, sides, weight_ref, gain_ref, out_ref, state_ref, product_ref=None, square_ref=None):
    lane = lax.broadcasted_iota(jnp.int32, (ROWS, 128), 1) // ROWS
    squares = [[None] * 3 for _ in blocks]
    for k in range(3):
        total = None if product_ref is None else product_ref[k]
        sums = None if square_ref is None else square_ref[:, k : k + 1]
        for refs, side in sides:
            at = 0
            for ref in refs:
                rows = ref.shape[0] * ROWS
                state_ref[at : at + rows, :] = ref[:, k].reshape(rows, HALF)
                at += rows
            states = state_ref[...]
            product = jnp.dot(states, weight_ref[k, half_of(side), :], preferred_element_type=F32)
            plain = states.astype(F32) * (1.0 / gain_ref[pl.ds(k, 1), half_of(side)])
            square = jnp.sum(plain * plain, axis=1, keepdims=True)
            total = product if total is None else total + product
            sums = square if sums is None else sums + square
        total = total.astype(BF)
        for i, block in enumerate(blocks):
            rows = slice(i * ROWS, (i + 1) * ROWS)
            squares[i][k] = sums[rows]
            for column in range(4):
                at = pl.multiple_of((k * 4 + column) * 32 + lax.rem(block, 2) * ROWS, ROWS)
                out_ref[block // 2, pl.ds(at, ROWS), :] = total[rows, column * 128 : (column + 1) * 128]
    for i, block in enumerate(blocks):
        packed = out_ref[block // 2, 384:400, :].astype(F32)
        for k in range(3):
            packed = jnp.where(lane == 2 * k + lax.rem(block, 2), squares[i][k], packed)
        out_ref[block // 2, 384:400, :] = packed.astype(BF)


def early_kernel(middle, middle_other, weight_ref, gain_ref, out_ref, state_ref):
    core = lax.axis_index(CORE)
    out_ref[:, 384:400, :] = jnp.zeros((8, ROWS, 128), BF)
    sides = (((middle,), core), ((middle_other,), 1 - core))
    join(blocks_of()[0], sides, weight_ref, gain_ref, out_ref, state_ref)


def last_mine_kernel(last, weight_ref, gain_ref, product_ref, square_ref, state_ref):
    lane = lax.broadcasted_iota(jnp.int32, square_ref.shape, 1)
    side = half_of(lax.axis_index(CORE))
    squares = jnp.zeros(square_ref.shape, F32)
    for k in range(3):
        state_ref[...] = last[:, k].reshape(state_ref.shape)
        states = state_ref[...]
        product_ref[k] = jnp.dot(states, weight_ref[k, side, :], preferred_element_type=F32)
        plain = states.astype(F32) * (1.0 / gain_ref[pl.ds(k, 1), side])
        squares = jnp.where(lane == k, jnp.sum(plain * plain, axis=1, keepdims=True), squares)
    square_ref[...] = squares


def last_kernel(early_ref, last_other, product_ref, square_ref, weight_ref, gain_ref, out_ref, state_ref):
    del early_ref
    sides = (((last_other,), 1 - lax.axis_index(CORE)),)
    join(blocks_of()[1], sides, weight_ref, gain_ref, out_ref, state_ref, product_ref, square_ref)


def scale_kernel(parts_ref, out_ref):
    squares = parts_ref[0, 384:400, :].astype(F32)
    for piece in range(1, 8):
        squares = squares + parts_ref[piece, 384:400, :].astype(F32)
    scale = lax.rsqrt(squares / D + EPS)
    for h in range(2):
        for column in range(4):
            joined = None
            for k in range(3):
                rows = pl.ds((k * 4 + column) * 32 + h * ROWS, ROWS)
                total = parts_ref[0, rows, :].astype(F32)
                for piece in range(1, 8):
                    total = total + parts_ref[piece, rows, :].astype(F32)
                at = ROWS * (2 * k + h)
                total = total * scale[:, at : at + 1]
                joined = total if joined is None else joined + total
            joined = joined.astype(BF)
            for copy in range(8):
                out_ref[copy, h * ROWS : (h + 1) * ROWS, column * 128 : (column + 1) * 128] = joined


def swap(a, axis):
    return lax.ppermute(a, axis, [(0, 1), (1, 0)])


def along(a, step):
    return lax.ppermute(a, Z, [(i, (i + step) % 8) for i in range(8)])


def exchange(a, axes):
    return lax.all_to_all(a, axes, 0, 0, tiled=True)


def reduce_two(ends, middle):
    return exchange(ends, (ZP, ZQ)), middle


def reduce_three(ends, middle):
    parts = exchange(jnp.concatenate([ends, middle[:, None]], axis=1), (ZP, ZQ))
    return parts[:, :2], parts[:, 2]


def states(count):
    return ((count, 3, ROWS, HALF), BF, pltpu.VMEM)


def shards(layer_deltas, tap_layers, norm_gain, fc_weight):
    raw = ((2, 128, HALF), BF, pltpu.VMEM)
    sources = [pltpu.with_memory_space_constraint(a, pltpu.HBM) for a in (tap_layers, layer_deltas, norm_gain)]
    sent = call(load_other_kernel, raw, [HBM], sources[1], scratch=[pltpu.SemaphoreType.DMA])
    own, taps, gain, three = call(
        load_kernel,
        [
            raw,
            (tap_layers.shape, jnp.int32, pltpu.SMEM),
            (norm_gain.shape, F32, pltpu.VMEM),
            ((1,), jnp.int32, pltpu.SMEM),
        ],
        [HBM] * 3 + [ANY],
        *sources,
        sent,
        scratch=[pltpu.SemaphoreType.DMA((3,))],
    )
    ends, middle = call(
        pair_kernel,
        [((8, 2, ROWS, HALF), BF, pltpu.VMEM), ((8, ROWS, HALF), BF, pltpu.VMEM)],
        [SMEM, VMEM, VMEM],
        taps,
        own,
        swap(sent, CORE),
    )
    ends, middle = lax.cond(three[0] != 0, reduce_three, reduce_two, ends, middle)
    piece = call(tapped_kernel, states(1), [SMEM, VMEM, VMEM, VMEM], taps, ends, middle, gain)
    below, above = along(piece, 2), along(piece, -2)
    near = swap(piece, LO)
    pack = functools.partial(pack_kernel, 3)
    right = call(pack, states(3), [VMEM] * 3, piece, below, near)
    left = call(pack, states(3), [VMEM] * 3, piece, above, near)
    across = call(functools.partial(pack_kernel, 2), states(2), [VMEM] * 2, above, below)
    half = ((1, 3, ROWS, HALF // 2), BF, pltpu.VMEM)
    up, down = call(halves_kernel, [half] * 2, [VMEM] * 2, above, below)
    weight = call(
        fetch_kernel,
        (fc_weight.shape, BF, pltpu.VMEM),
        [HBM, ANY],
        pltpu.with_memory_space_constraint(fc_weight, pltpu.HBM),
        across,
        scratch=[pltpu.SemaphoreType.DMA],
    )
    first = (swap(across, LO), along(right, 1), along(left, -1), along(up, -2), along(down, 2), weight)
    across, from_left, from_right, up, down, weight = lax.optimization_barrier(first)
    left, right = call(ends_kernel, [states(1)] * 2, [VMEM], across)
    far = call(far_kernel, states(1), [VMEM] * 2, up, down)
    far_left, far_right, far_across = along(right, 1), along(left, -1), swap(far, LO)
    pack = functools.partial(pack_kernel, 8)
    pieces = (piece, below, above, near, from_left, from_right, across, far)
    middle = call(pack, states(13), [VMEM] * 8, *pieces)
    payload = ((8, 400, 128), BF, pltpu.VMEM)
    partial = call(
        early_kernel,
        payload,
        [VMEM] * 4,
        middle,
        swap(middle, CORE),
        weight,
        gain,
        flops=2 * 208 * 6144 * 512,
        scratch=[pltpu.VMEM((208, HALF), BF)],
    )
    pack = functools.partial(pack_kernel, 3)
    last = call(pack, states(3), [VMEM] * 3 + [ANY], far_across, far_left, far_right, partial)
    product, square = call(
        last_mine_kernel,
        [((3, 48, 512), F32, pltpu.VMEM), ((48, 128), F32, pltpu.VMEM)],
        [VMEM] * 3,
        last,
        weight,
        gain,
        flops=48 * 6144 * 512,
        scratch=[pltpu.VMEM((48, HALF), BF)],
    )
    partial = call(
        last_kernel,
        payload,
        [VMEM] * 6,
        partial,
        swap(last, CORE),
        product,
        square,
        weight,
        gain,
        flops=48 * 6144 * 512,
        scratch=[pltpu.VMEM((48, HALF), BF)],
        alias={0: 0},
    )
    partial = exchange(partial, (X, HI))
    joined = call(scale_kernel, ((8, 32, 512), BF, pltpu.VMEM), [VMEM], partial)
    return exchange(joined, (X, HI)).reshape(256, 512)


def solution(mesh):
    fine = Mesh(mesh.devices.reshape(4, 2, 2, 2, 4, 2), (ZQ, ZP, CORE, HI, X, LO))
    section, tensor = (ZQ, ZP, CORE), (HI, X)
    in_specs = (P(section, LO, tensor), P(), P(None, tensor), P(None, tensor, (*section, LO)))
    out_specs = P(None, (*section, LO))
    return jax.shard_map(shards, mesh=fine, in_specs=in_specs, out_specs=out_specs, check_vma=False)
```

```python
import functools

import jax
import jax.numpy as jnp
from jax import lax
from jax.experimental import pallas as pl
from jax.experimental.pallas import tpu as pltpu
from jax.sharding import Mesh, PartitionSpec as P

D = 16384
EPS = 1e-05
ZQ, ZP, CORE, HI, X, LO = "zq", "zp", "core", "hi", "x", "lo"
Z = (ZQ, ZP)
BF, F32 = jnp.bfloat16, jnp.float32
ROWS = 16
HALF = 1024
MIB = 1 << 20

VMEM = pl.BlockSpec(memory_space=pltpu.VMEM)
SMEM = pl.BlockSpec(memory_space=pltpu.SMEM)
HBM = pl.BlockSpec(memory_space=pltpu.HBM)
ANY = pl.BlockSpec(memory_space=pl.ANY)


def call(kernel, shapes, specs, *args, flops=0, limit=24, scratch=(), alias=None):
    size = sum(a.size * a.dtype.itemsize for a in args)
    single = not isinstance(shapes, list)
    shapes = [shapes] if single else shapes
    out = pl.pallas_call(
        kernel,
        out_shape=[space(shape, kind) for shape, kind, space in shapes],
        in_specs=specs,
        out_specs=[pl.BlockSpec(memory_space=space) for _, _, space in shapes],
        scratch_shapes=list(scratch),
        input_output_aliases=alias or {},
        cost_estimate=pl.CostEstimate(flops=flops, bytes_accessed=size, transcendentals=0),
        compiler_params=pltpu.CompilerParams(vmem_limit_bytes=limit * MIB),
    )(*args)
    return out[0] if single else out


def half_of(core):
    return pl.ds(pl.multiple_of(core * HALF, HALF), HALF)


def segment(layer, tap_ref):
    return (layer > tap_ref[0]).astype(jnp.int32) + (layer > tap_ref[1]).astype(jnp.int32)


def load_other_kernel(delta_hbm, other_ref, sem):
    copy = pltpu.make_async_copy(delta_hbm.at[:, :, half_of(1 - lax.axis_index(CORE))], other_ref, sem)
    copy.start()
    copy.wait()


def load_kernel(tap_hbm, delta_hbm, gain_hbm, after_ref, mine_ref, tap_ref, gain_ref, three_ref, sems):
    del after_ref
    core = lax.axis_index(CORE)
    pairs = (
        (delta_hbm.at[:, :, half_of(core)], mine_ref),
        (tap_hbm, tap_ref),
        (gain_hbm, gain_ref),
    )
    copies = [pltpu.make_async_copy(a, b, sems.at[i]) for i, (a, b) in enumerate(pairs)]
    for copy in copies:
        copy.start()
    for copy in copies:
        copy.wait()
    three_ref[0] = (tap_ref[0] // 4 == tap_ref[1] // 4).astype(jnp.int32)


def pair_kernel(tap_ref, mine_ref, other_ref, ends_ref, middle_ref):
    core = lax.axis_index(CORE)
    first = (lax.axis_index(ZQ) * 2 + lax.axis_index(ZP)) * 4
    head, tail = segment(first, tap_ref), segment(first + 3, tap_ref)
    weights = []
    for side in (core, 1 - core):
        for j in range(2):
            at = segment(first + 2 * side + j, tap_ref)
            in_head = at == head
            in_tail = jnp.logical_and(at == tail, tail != head)
            between = jnp.logical_not(jnp.logical_or(in_head, in_tail))
            weights.append([jnp.where(w, 1.0, 0.0).astype(F32) for w in (in_head, in_tail, between)])
    for piece in range(8):
        rows = slice(piece * ROWS, (piece + 1) * ROWS)
        layers = [ref[j, rows].astype(F32) for ref in (mine_ref, other_ref) for j in range(2)]
        sums = []
        for part in range(3):
            terms = [layer * weight[part] for layer, weight in zip(layers, weights)]
            sums.append(((terms[0] + terms[1]) + (terms[2] + terms[3])).astype(BF))
        ends_ref[piece, 0] = sums[0]
        ends_ref[piece, 1] = sums[1]
        middle_ref[piece] = sums[2]


def tapped_kernel(tap_ref, ends_ref, middle_ref, gain_ref, out_ref):
    columns = half_of(lax.axis_index(CORE))
    between = middle_ref[0].astype(F32)
    for chip in range(1, 8):
        between = between + middle_ref[chip].astype(F32)
    for k in range(3):
        state = between if k else jnp.zeros_like(between)
        for slot in range(8):
            chip = 2 * (slot % 4) + slot // 4
            for end in range(2):
                inside = jnp.where(4 * chip + 3 * end <= tap_ref[k], 1.0, 0.0).astype(F32)
                state = state + ends_ref[slot, end].astype(F32) * inside
        out_ref[0, k] = (state * gain_ref[pl.ds(k, 1), columns]).astype(BF)


def blocks_of():
    z = 2 * lax.axis_index(ZQ) + lax.axis_index(ZP)
    mine = lax.axis_index(LO) * 8

    def block(group, step):
        chip = lax.rem(z + step, 8)
        return group + lax.rem(chip, 2) * 4 + chip // 2

    yours = 8 - mine
    early = [block(mine, step) for step in (0, 6, 2)] + [block(yours, 0)]
    early += [block(mine, 7), block(mine, 5), block(yours, 7)]
    early += [block(mine, 1), block(mine, 3), block(yours, 1)]
    early += [block(yours, 2), block(yours, 6), block(mine, 4)]
    return early, [block(yours, 4), block(yours, 5), block(yours, 3)]


def halves_kernel(above, below, up_ref, down_ref):
    up_ref[...] = above[:, :, :, : HALF // 2]
    down_ref[...] = below[:, :, :, HALF // 2 :]


def far_kernel(up, down, far_ref):
    far_ref[:, :, :, : HALF // 2] = up[...]
    far_ref[:, :, :, HALF // 2 :] = down[...]


def pack_kernel(count, *refs):
    out_ref = refs[-1]
    at = 0
    for ref in refs[:count]:
        out_ref[at : at + ref.shape[0]] = ref[...]
        at += ref.shape[0]


def ends_kernel(across_ref, left_ref, right_ref):
    left_ref[0] = across_ref[0]
    right_ref[0] = across_ref[1]


def fetch_kernel(weight_hbm, after_ref, weight_ref, sem):
    del after_ref
    copy = pltpu.make_async_copy(weight_hbm, weight_ref, sem)
    copy.start()
    copy.wait()


def join(blocks, sides, weight_ref, gain_ref, out_ref, state_ref, product_ref=None, square_ref=None):
    lane = lax.broadcasted_iota(jnp.int32, (ROWS, 128), 1) // ROWS
    squares = [[None] * 3 for _ in blocks]
    for k in range(3):
        total = None if product_ref is None else product_ref[k]
        sums = None if square_ref is None else square_ref[:, k : k + 1]
        for refs, side in sides:
            at = 0
            for ref in refs:
                rows = ref.shape[0] * ROWS
                state_ref[at : at + rows, :] = ref[:, k].reshape(rows, HALF)
                at += rows
            states = state_ref[...]
            product = jnp.dot(states, weight_ref[k, half_of(side), :], preferred_element_type=F32)
            plain = states.astype(F32) * (1.0 / gain_ref[pl.ds(k, 1), half_of(side)])
            square = jnp.sum(plain * plain, axis=1, keepdims=True)
            total = product if total is None else total + product
            sums = square if sums is None else sums + square
        total = total.astype(BF)
        for i, block in enumerate(blocks):
            rows = slice(i * ROWS, (i + 1) * ROWS)
            squares[i][k] = sums[rows]
            for column in range(4):
                at = pl.multiple_of((k * 4 + column) * 32 + lax.rem(block, 2) * ROWS, ROWS)
                out_ref[block // 2, pl.ds(at, ROWS), :] = total[rows, column * 128 : (column + 1) * 128]
    for i, block in enumerate(blocks):
        packed = out_ref[block // 2, 384:400, :].astype(F32)
        for k in range(3):
            packed = jnp.where(lane == 2 * k + lax.rem(block, 2), squares[i][k], packed)
        out_ref[block // 2, 384:400, :] = packed.astype(BF)


def early_kernel(middle, middle_other, weight_ref, gain_ref, out_ref, state_ref):
    core = lax.axis_index(CORE)
    out_ref[:, 384:400, :] = jnp.zeros((8, ROWS, 128), BF)
    sides = (((middle,), core), ((middle_other,), 1 - core))
    join(blocks_of()[0], sides, weight_ref, gain_ref, out_ref, state_ref)


def last_mine_kernel(across, last, weight_ref, gain_ref, product_ref, square_ref, state_ref):
    lane = lax.broadcasted_iota(jnp.int32, square_ref.shape, 1)
    side = half_of(lax.axis_index(CORE))
    squares = jnp.zeros(square_ref.shape, F32)
    for k in range(3):
        state_ref[:ROWS, :] = across[0, k]
        state_ref[ROWS:, :] = last[:, k].reshape(2 * ROWS, HALF)
        states = state_ref[...]
        product_ref[k] = jnp.dot(states, weight_ref[k, side, :], preferred_element_type=F32)
        plain = states.astype(F32) * (1.0 / gain_ref[pl.ds(k, 1), side])
        squares = jnp.where(lane == k, jnp.sum(plain * plain, axis=1, keepdims=True), squares)
    square_ref[...] = squares


def last_kernel(early_ref, across_other, last_other, product_ref, square_ref, weight_ref, gain_ref, out_ref, state_ref):
    del early_ref
    sides = (((across_other, last_other), 1 - lax.axis_index(CORE)),)
    join(blocks_of()[1], sides, weight_ref, gain_ref, out_ref, state_ref, product_ref, square_ref)


def scale_kernel(parts_ref, out_ref):
    squares = parts_ref[0, 384:400, :].astype(F32)
    for piece in range(1, 8):
        squares = squares + parts_ref[piece, 384:400, :].astype(F32)
    scale = lax.rsqrt(squares / D + EPS)
    for h in range(2):
        for column in range(4):
            joined = None
            for k in range(3):
                rows = pl.ds((k * 4 + column) * 32 + h * ROWS, ROWS)
                total = parts_ref[0, rows, :].astype(F32)
                for piece in range(1, 8):
                    total = total + parts_ref[piece, rows, :].astype(F32)
                at = ROWS * (2 * k + h)
                total = total * scale[:, at : at + 1]
                joined = total if joined is None else joined + total
            joined = joined.astype(BF)
            for copy in range(8):
                out_ref[copy, h * ROWS : (h + 1) * ROWS, column * 128 : (column + 1) * 128] = joined


def swap(a, axis):
    return lax.ppermute(a, axis, [(0, 1), (1, 0)])


def along(a, step):
    return lax.ppermute(a, Z, [(i, (i + step) % 8) for i in range(8)])


def exchange(a, axes):
    return lax.all_to_all(a, axes, 0, 0, tiled=True)


def reduce_two(ends, middle):
    return exchange(ends, (ZP, ZQ)), middle


def reduce_three(ends, middle):
    parts = exchange(jnp.concatenate([ends, middle[:, None]], axis=1), (ZP, ZQ))
    return parts[:, :2], parts[:, 2]


def states(count):
    return ((count, 3, ROWS, HALF), BF, pltpu.VMEM)


def shards(layer_deltas, tap_layers, norm_gain, fc_weight):
    raw = ((2, 128, HALF), BF, pltpu.VMEM)
    sources = [pltpu.with_memory_space_constraint(a, pltpu.HBM) for a in (tap_layers, layer_deltas, norm_gain)]
    sent = call(load_other_kernel, raw, [HBM], sources[1], scratch=[pltpu.SemaphoreType.DMA])
    own, taps, gain, three = call(
        load_kernel,
        [
            raw,
            (tap_layers.shape, jnp.int32, pltpu.SMEM),
            (norm_gain.shape, F32, pltpu.VMEM),
            ((1,), jnp.int32, pltpu.SMEM),
        ],
        [HBM] * 3 + [ANY],
        *sources,
        sent,
        scratch=[pltpu.SemaphoreType.DMA((3,))],
    )
    ends, middle = call(
        pair_kernel,
        [((8, 2, ROWS, HALF), BF, pltpu.VMEM), ((8, ROWS, HALF), BF, pltpu.VMEM)],
        [SMEM, VMEM, VMEM],
        taps,
        own,
        swap(sent, CORE),
    )
    ends, middle = lax.cond(three[0] != 0, reduce_three, reduce_two, ends, middle)
    piece = call(tapped_kernel, states(1), [SMEM, VMEM, VMEM, VMEM], taps, ends, middle, gain)
    below, above = along(piece, 2), along(piece, -2)
    near = swap(piece, LO)
    pack = functools.partial(pack_kernel, 3)
    right = call(pack, states(3), [VMEM] * 3, piece, below, near)
    left = call(pack, states(3), [VMEM] * 3, piece, above, near)
    across = call(functools.partial(pack_kernel, 2), states(2), [VMEM] * 2, above, below)
    half = ((1, 3, ROWS, HALF // 2), BF, pltpu.VMEM)
    up, down = call(halves_kernel, [half] * 2, [VMEM] * 2, above, below)
    weight = call(
        fetch_kernel,
        (fc_weight.shape, BF, pltpu.VMEM),
        [HBM, ANY],
        pltpu.with_memory_space_constraint(fc_weight, pltpu.HBM),
        across,
        scratch=[pltpu.SemaphoreType.DMA],
    )
    first = (swap(across, LO), along(right, 1), along(left, -1), along(up, -2), along(down, 2), weight)
    across, from_left, from_right, up, down, weight = lax.optimization_barrier(first)
    left, right = call(ends_kernel, [states(1)] * 2, [VMEM], across)
    far = call(far_kernel, states(1), [VMEM] * 2, up, down)
    far_left, far_right, far_across = along(right, 1), along(left, -1), swap(far, LO)
    pack = functools.partial(pack_kernel, 8)
    pieces = (piece, below, above, near, from_left, from_right, across, far)
    middle = call(pack, states(13), [VMEM] * 8, *pieces)
    payload = ((8, 400, 128), BF, pltpu.VMEM)
    partial = call(
        early_kernel,
        payload,
        [VMEM] * 4,
        middle,
        swap(middle, CORE),
        weight,
        gain,
        flops=2 * 208 * 6144 * 512,
        scratch=[pltpu.VMEM((208, HALF), BF)],
    )
    pack = functools.partial(pack_kernel, 2)
    last = call(pack, states(2), [VMEM] * 2 + [ANY], far_left, far_right, partial)
    product, square = call(
        last_mine_kernel,
        [((3, 48, 512), F32, pltpu.VMEM), ((48, 128), F32, pltpu.VMEM)],
        [VMEM] * 4,
        far_across,
        last,
        weight,
        gain,
        flops=48 * 6144 * 512,
        scratch=[pltpu.VMEM((48, HALF), BF)],
    )
    partial = call(
        last_kernel,
        payload,
        [VMEM] * 7,
        partial,
        swap(far_across, CORE),
        swap(last, CORE),
        product,
        square,
        weight,
        gain,
        flops=48 * 6144 * 512,
        scratch=[pltpu.VMEM((48, HALF), BF)],
        alias={0: 0},
    )
    partial = exchange(partial, (X, HI))
    joined = call(scale_kernel, ((8, 32, 512), BF, pltpu.VMEM), [VMEM], partial)
    return exchange(joined, (X, HI)).reshape(256, 512)


def solution(mesh):
    fine = Mesh(mesh.devices.reshape(4, 2, 2, 2, 4, 2), (ZQ, ZP, CORE, HI, X, LO))
    section, tensor = (ZQ, ZP, CORE), (HI, X)
    in_specs = (P(section, LO, tensor), P(), P(None, tensor), P(None, tensor, (*section, LO)))
    out_specs = P(None, (*section, LO))
    return jax.shard_map(shards, mesh=fine, in_specs=in_specs, out_specs=out_specs, check_vma=False)
```
